128 devices in a mesh: slab: 8 (over y, core), inner: 16 (over z, x).
Axes of the slice: x: 4, y: 4, z: 4, core: 2. Of those that a mesh axis runs over, the one named last changes fastest.
Arguments:
- x_in: bfloat16 [32768, 16384], P(('slab', 'inner')), may hold values from -6 to 6
- bc_in: bfloat16 [32768, 4096], P(('slab', 'inner')), may hold values from -6 to 6
- dt_raw: bfloat16 [32768, 256], P(('slab', 'inner')), may hold values from -6.7 to -4.3
- dt_bias: float32 [256], replicated, may hold values from -0.5 to 0.5
- a_log: float32 [256], replicated, may hold values from -8 to 0, as said below
- d_skip: float32 [256], replicated, may hold values from 0.5 to 1.5
- conv_x_weight: float32 [4, 16384], replicated, may hold values from -3 to 3
- conv_x_bias: float32 [16384], replicated, may hold values from -3 to 3
- conv_bc_weight: float32 [4, 4096], replicated, may hold values from -3 to 3
- conv_bc_bias: float32 [4096], replicated, may hold values from -3 to 3
Outputs:
- y_out: bfloat16 [32768, 16384], P('slab', 'inner')
The draws below stay inside these ranges and needn't reach their ends.
Inputs may be any that keep to these rules, and one draw needn't show every extreme that they name: `a_log`: per-head logarithm of the decay rate.
All inputs are finite; a program needn't handle non-finite values.
Results may differ from the reference program's by a relative error of at most 0.0034.
Values may be sent and summed in bfloat16 or wider, within the bound.
A program may use at most 256 MiB of HBM per device.

```python
import jax
import jax.numpy as jnp
from jax import lax

HEADS = 256
HEADDIM = 64
STATE = 256
GROUPS = 8
CONV = 4
SPAN = 256
INNER = 16384
SLAB_TOK = 4096
TOKENS = 32768
N_SLAB = 8


def draw_a_log(key, part):
    picked = jax.random.permutation(jax.random.fold_in(key, 11), HEADS)
    spread = jax.random.uniform(jax.random.fold_in(key, 12), (HEADS,), jnp.float32)
    fast_count = HEADS // 2
    fast_heads = picked < fast_count
    fast_rate = -1.6 + spread * 1.2
    slow_rate = jnp.log(0.2) + spread * jnp.log(5.0) - jnp.log(0.0041 * TOKENS)
    return jnp.where(fast_heads, fast_rate, slow_rate).astype(jnp.float32)


def draw_dt_raw(key, part):
    rough = jax.random.uniform(jax.random.fold_in(key, 21), (TOKENS, HEADS), jnp.float32, -0.8, 0.8)
    blocks = jax.random.uniform(jax.random.fold_in(key, 22), (TOKENS // SPAN, 1), jnp.float32, -0.35, 0.35)
    values = -5.5 + rough + jnp.repeat(blocks, SPAN, axis=0)
    return values.astype(jnp.bfloat16)


def block_scale(stream_key, extent, shards, least, top_value):
    factor_of, own = 1.0, jax.random.fold_in(stream_key, 6)
    for axis_at, shards_of in shards:
        draws = jnp.exp(jax.random.uniform(jax.random.fold_in(own, axis_at), (shards_of,), jnp.float32, least / len(shards), top_value / len(shards)))
        factor_of = factor_of * jnp.repeat(draws, extent[axis_at] // shards_of).reshape([-1 if axis == axis_at else 1 for axis in range(len(extent))])
    return factor_of


def gaussian(stream_key, extent, scale, limit, cuts=(), kind=jnp.bfloat16):
    array = scale * jax.random.normal(stream_key, extent, jnp.float32)
    if cuts:
        array = array * block_scale(stream_key, extent, cuts, -0.22, 0.18)
    return jnp.clip(array, -limit, limit).astype(kind)


def setup_inputs(seed: int = 0) -> dict:
    key_of = jax.random.split(jax.random.key(seed), 11)
    return {
        "x_in": gaussian(key_of[0], (TOKENS, INNER), 1.0, 6.0, ((0, 128),)),
        "bc_in": gaussian(key_of[1], (TOKENS, 2 * GROUPS * STATE), 1.0, 6.0, ((0, 128),)),
        "dt_raw": draw_dt_raw(jax.random.fold_in(key_of[10], 71), 0),
        "dt_bias": jnp.clip(jax.random.uniform(key_of[3], (HEADS,), jnp.float32, -0.5, 0.5), -0.5, 0.5),
        "a_log": draw_a_log(jax.random.fold_in(key_of[10], 71), 0),
        "d_skip": jnp.clip(jax.random.uniform(key_of[5], (HEADS,), jnp.float32, 0.5, 1.5), 0.5, 1.5),
        "conv_x_weight": gaussian(key_of[6], (CONV, INNER), CONV ** -0.5, 3.0, (), jnp.float32),
        "conv_x_bias": gaussian(key_of[7], (INNER,), 0.5, 3.0, (), jnp.float32),
        "conv_bc_weight": gaussian(key_of[8], (CONV, 2 * GROUPS * STATE), CONV ** -0.5, 3.0, (), jnp.float32),
        "conv_bc_bias": gaussian(key_of[9], (2 * GROUPS * STATE,), 0.5, 3.0, (), jnp.float32),
    }


def causal_conv(row_block, before, weight, conv_bias):
    kernel_len = weight.shape[0]
    length = row_block.shape[0]
    padded = jnp.concatenate([before, row_block], axis=0).astype(jnp.float32)
    summed = conv_bias[None, :] + weight[0][None, :] * padded[0:length]
    for offset in range(1, kernel_len):
        summed = summed + weight[offset][None, :] * padded[offset:offset + length]
    return jax.nn.silu(summed).astype(jnp.bfloat16)


def span_step(state, pieces):
    x_span, b_span, c_span, dt_span, da_span = pieces
    cumul = jnp.cumsum(da_span, axis=0).T
    size_q = cumul.shape[1]
    row_ids = lax.broadcasted_iota(jnp.int32, (size_q, size_q), 0)
    col_ids = lax.broadcasted_iota(jnp.int32, (size_q, size_q), 1)
    gaps = cumul[:, :, None] - cumul[:, None, :]
    decays = jnp.where((row_ids >= col_ids)[None], jnp.exp(jnp.minimum(gaps, 0.0)), 0.0)
    scores = jnp.dot(c_span, b_span.T, preferred_element_type=jnp.float32)
    mixing = (decays * scores[None] * dt_span.T[:, None, :]).astype(jnp.bfloat16)
    y_intra = jnp.einsum("hts,shp->thp", mixing.astype(jnp.float32), x_span.astype(jnp.float32))
    y_inter = jnp.einsum("tn,hnp->thp", c_span.astype(jnp.float32), state.astype(jnp.bfloat16).astype(jnp.float32))
    y_inter = y_inter * jnp.exp(cumul.T)[:, :, None]
    weights_end = (jnp.exp(cumul[:, -1:] - cumul) * dt_span.T).T
    scaled = (x_span.astype(jnp.float32) * weights_end[:, :, None]).astype(jnp.bfloat16)
    contrib = jnp.einsum("sn,shp->hnp", b_span.astype(jnp.float32), scaled.astype(jnp.float32))
    new_state = jnp.exp(cumul[:, -1])[:, None, None] * state + contrib
    return new_state, y_intra + y_inter


def slab_core(x_rows, b_rows, c_rows, dt_rows, da_rows):
    length = x_rows.shape[0]
    head_count = dt_rows.shape[1]
    span_count = length // SPAN
    inputs = (x_rows.reshape(span_count, SPAN, head_count, HEADDIM),
              b_rows.reshape(span_count, SPAN, STATE),
              c_rows.reshape(span_count, SPAN, STATE),
              dt_rows.reshape(span_count, SPAN, head_count),
              da_rows.reshape(span_count, SPAN, head_count))
    zero_state = jnp.zeros((head_count, STATE, HEADDIM), jnp.float32)
    end_state, outputs = lax.scan(span_step, zero_state, inputs)
    return outputs.reshape(length, head_count * HEADDIM), end_state


def reference(x_in, bc_in, dt_raw, dt_bias, a_log, d_skip, conv_x_weight, conv_x_bias, conv_bc_weight, conv_bc_bias):
    edge = CONV - 1
    bc_width = 2 * GROUPS * STATE
    x_slabs = x_in.reshape(N_SLAB, SLAB_TOK, INNER)
    bc_slabs = bc_in.reshape(N_SLAB, SLAB_TOK, bc_width)
    x_before = jnp.concatenate([jnp.zeros((1, edge, INNER), jnp.bfloat16), x_slabs[:-1, SLAB_TOK - edge:]], axis=0)
    bc_before = jnp.concatenate([jnp.zeros((1, edge, bc_width), jnp.bfloat16), bc_slabs[:-1, SLAB_TOK - edge:]], axis=0)
    dt_all = jax.nn.softplus(dt_raw.astype(jnp.float32) + dt_bias[None, :])
    da_all = dt_all * (-jnp.exp(a_log))[None, :]
    dt_slabs = dt_all.reshape(N_SLAB, SLAB_TOK, HEADS)
    da_slabs = da_all.reshape(N_SLAB, SLAB_TOK, HEADS)
    per_group = HEADS // GROUPS
    skip_cols = jnp.repeat(d_skip, HEADDIM)

    def one_slab(incoming, pieces):
        x_rows, x_prev, bc_rows, bc_prev, dt_rows, da_rows = pieces
        x_conv = causal_conv(x_rows, x_prev, conv_x_weight, conv_x_bias)
        bc_conv = causal_conv(bc_rows, bc_prev, conv_bc_weight, conv_bc_bias)
        y_parts = []
        end_parts = []
        for group_id in range(GROUPS):
            first = group_id * per_group
            y_part, end_part = slab_core(
                x_conv[:, first * HEADDIM:(first + per_group) * HEADDIM],
                bc_conv[:, group_id * STATE:(group_id + 1) * STATE],
                bc_conv[:, (GROUPS + group_id) * STATE:(GROUPS + group_id + 1) * STATE],
                dt_rows[:, first:first + per_group],
                da_rows[:, first:first + per_group])
            y_parts.append(y_part)
            end_parts.append(end_part)
        y_local = jnp.concatenate(y_parts, axis=1)
        end_local = jnp.concatenate(end_parts, axis=0)
        cum_slab = jnp.cumsum(da_rows, axis=0)
        c_groups = bc_conv[:, GROUPS * STATE:].reshape(SLAB_TOK, GROUPS, STATE).astype(jnp.float32)
        state_groups = incoming.astype(jnp.bfloat16).astype(jnp.float32).reshape(GROUPS, per_group, STATE, HEADDIM)
        carried = jnp.einsum("tgn,ghnp->tghp", c_groups, state_groups).reshape(SLAB_TOK, HEADS, HEADDIM)
        carried = carried * jnp.exp(cum_slab)[:, :, None]
        y_slab = y_local + carried.reshape(SLAB_TOK, INNER) + skip_cols[None, :] * x_conv.astype(jnp.float32)
        outgoing = jnp.exp(cum_slab[-1])[:, None, None] * incoming + end_local
        return outgoing, y_slab.astype(jnp.bfloat16)

    start_state = jnp.zeros((HEADS, STATE, HEADDIM), jnp.float32)
    last_state, y_all = lax.scan(one_slab, start_state, (x_slabs, x_before, bc_slabs, bc_before, dt_slabs, da_slabs))
    return y_all.reshape(TOKENS, INNER)
```

```python
import jax
import jax.numpy as jnp
from jax import lax
from jax.experimental import pallas as pl
from jax.experimental.pallas import tpu as pltpu
from jax.sharding import PartitionSpec as P

HEADS = 256
HEADDIM = 64
STATE = 256
GROUPS = 8
SPAN = 256
N_SLAB = 8
N_INNER = 16
CH = 1024
NH = 16
PIECES = 4
COLS = CH // PIECES
EDGE = 16
SUB = 64
MESH = pl.DeviceIdType.MESH
ORDER = (
    (2, 2), (1, 0), (0, 3), (3, 1), (2, 1), (0, 1), (3, 0), (1, 3),
    (1, 2), (2, 0), (3, 3), (0, 2), (1, 1), (2, 3), (3, 2),
)
N_PEER = len(ORDER)
F32 = jnp.float32
BF16 = jnp.bfloat16


def dot(a, b):
    return jnp.dot(a, b, preferred_element_type=F32)


def conv_silu(rows, weight, bias):
    full = rows.astype(F32)
    n = rows.shape[0] - EDGE
    acc = bias
    for k in range(4):
        start = EDGE - 3 + k
        acc = acc + weight[k : k + 1, :] * full[start : start + n]
    half = 0.5 * acc
    return (half + half * jnp.tanh(half)).astype(BF16)


def body(
    x_ref, bc_ref, dt_ref, head_ref, wx_ref, bx_ref, wbc_ref, bbc_ref,
    out_ref,
    xbuf, bbuf, cbuf, dtbuf, dt_t, gm, cc, bt, coef, ew, ee, dec, ep, tot, skip, state, xs, xc, ebuf, arr, inc,
    xsend, xrecv, ssend, srecv, hsend, hrecv, tsend, trecv, esend, erecv, osem,
):
    slab = lax.axis_index("slab")
    me = lax.axis_index("inner")
    my_z, my_x = me // 4, lax.rem(me, 4)
    sign = 1 - 2 * lax.rem(slab, 2)
    peers = [
        lax.rem(my_z + sign * dz + 4, 4) * 4 + lax.rem(my_x + sign * dx + 4, 4)
        for dx, dz in ORDER
    ]
    halo_out = jnp.logical_and(me == N_INNER - 1, slab < N_SLAB - 1)

    barrier = pltpu.get_barrier_semaphore()
    for peer in peers:
        pl.semaphore_signal(barrier, inc=1, device_id=(slab, peer), device_id_type=MESH)
    for k in range(1, N_SLAB):

        @pl.when(slab >= k)
        def _():
            pl.semaphore_signal(barrier, inc=1, device_id=(slab - k, me), device_id_type=MESH)

    @pl.when(slab > 0)
    def _():
        pl.semaphore_signal(barrier, inc=1, device_id=(slab - 1, N_INNER - 1), device_id_type=MESH)

    pl.semaphore_wait(
        barrier, N_PEER + (N_SLAB - 1 - slab) + jnp.where(halo_out, N_INNER, 0)
    )

    def rows_of(j):
        return pl.ds(pl.multiple_of(EDGE + j * SPAN, EDGE), SPAN)

    def x_cols(d, p):
        return pl.ds(pl.multiple_of(d * CH + p * COLS, COLS), COLS)

    def bc_cols(d, which):
        return pl.ds(pl.multiple_of((d // 2 + which * GROUPS) * STATE, STATE), STATE)

    def remote(src, dst, send_sem, recv_sem, to):
        return pltpu.make_async_remote_copy(
            src, dst, send_sem, recv_sem, device_id=to, device_id_type=MESH
        )

    def bc_copy(n, which):
        buf = (bbuf, cbuf)[which]
        return remote(
            bc_ref.at[:, bc_cols(peers[n], which)], buf.at[rows_of(me)],
            ssend.at[which, n], srecv.at[which, me], (slab, peers[n]),
        )

    def dt_copy(n):
        return remote(
            dt_t.at[pl.ds(pl.multiple_of(peers[n] * NH, NH), NH)], dtbuf.at[me],
            ssend.at[2, n], srecv.at[2, me], (slab, peers[n]),
        )

    def x_copy(n, p):
        return remote(
            x_ref.at[:, x_cols(peers[n], p)], xbuf.at[p, rows_of(me)],
            xsend.at[p, n], xrecv.at[p, me], (slab, peers[n]),
        )

    def halo_copies(d):
        tail = pl.ds(SPAN - EDGE, EDGE)
        to = (slab + 1, d)
        return [
            remote(bc_ref.at[tail, bc_cols(d, 0)], bbuf.at[pl.ds(0, EDGE)], hsend.at[0, d], hrecv.at[0], to),
            remote(bc_ref.at[tail, bc_cols(d, 1)], cbuf.at[pl.ds(0, EDGE)], hsend.at[1, d], hrecv.at[1], to),
        ] + [
            remote(
                x_ref.at[tail, x_cols(d, p)], xbuf.at[p, pl.ds(0, EDGE)], hsend.at[2 + p, d], hrecv.at[2 + p], to
            )
            for p in range(PIECES)
        ]

    dt_t[...] = dt_ref[...].astype(F32).T.astype(BF16)
    for n in range(N_PEER):
        dt_copy(n).start()
    for n in range(N_PEER):
        for which in range(2):
            bc_copy(n, which).start()

    @pl.when(halo_out)
    def _():
        @pl.loop(0, N_INNER)
        def _(d):
            for copy in halo_copies(d):
                copy.start()

    own = [
        pltpu.make_async_copy(bc_ref.at[:, bc_cols(me, 0)], bbuf.at[rows_of(me)], srecv.at[0, me]),
        pltpu.make_async_copy(bc_ref.at[:, bc_cols(me, 1)], cbuf.at[rows_of(me)], srecv.at[1, me]),
        pltpu.make_async_copy(
            dt_t.at[pl.ds(pl.multiple_of(me * NH, NH), NH)], dtbuf.at[me], srecv.at[2, me]
        ),
    ] + [
        pltpu.make_async_copy(x_ref.at[:, x_cols(me, p)], xbuf.at[p, rows_of(me)], xrecv.at[p, me])
        for p in range(PIECES)
    ]
    for copy in own:
        copy.start()
    for p in range(PIECES):
        for n in range(N_PEER):
            x_copy(n, p).start()

    chan = lax.broadcasted_iota(jnp.int32, (128, CH), 1) // HEADDIM
    row = lax.broadcasted_iota(jnp.int32, (128, CH), 0)
    ew[...] = jnp.where((row < 2 * NH) & (lax.rem(row, NH) == chan), 1.0, 0.0).astype(BF16)
    ee[...] = jnp.where(
        (row >= 2 * NH) & (row < 4 * NH) & (lax.rem(row, NH) == chan), 1.0, 0.0
    ).astype(BF16)
    heads = head_ref[pl.ds(pl.multiple_of(me * NH, NH), NH), :]
    bias_col, rate_col, skip_col = heads[:, 0:1], -jnp.exp(heads[:, 1:2]), heads[:, 2:3]
    pick = lax.broadcasted_iota(jnp.int32, (NH, CH), 0) == (
        lax.broadcasted_iota(jnp.int32, (NH, CH), 1) // HEADDIM
    )
    skip[...] = jnp.sum(jnp.where(pick, skip_col, 0.0), axis=0, keepdims=True)
    ep[0] = jnp.ones((1, CH), F32)
    row_ids = lax.broadcasted_iota(jnp.int32, (SPAN, SPAN), 0)
    col_ids = lax.broadcasted_iota(jnp.int32, (SPAN, SPAN), 1)
    upto = jnp.where(row_ids <= col_ids, 1.0, 0.0).astype(F32)

    @pl.when(slab == 0)
    def _():
        bbuf[pl.ds(0, EDGE), :] = jnp.zeros((EDGE, STATE), BF16)
        cbuf[pl.ds(0, EDGE), :] = jnp.zeros((EDGE, STATE), BF16)
        for p in range(PIECES):
            xbuf[p, pl.ds(0, EDGE), :] = jnp.zeros((EDGE, COLS), BF16)

    @pl.when(slab > 0)
    def _():
        for k, buf in enumerate((bbuf, cbuf)):
            edge = buf.at[pl.ds(0, EDGE)]
            pltpu.make_async_copy(edge, edge, hrecv.at[k]).wait()
        for p in range(PIECES):
            edge = xbuf.at[p, pl.ds(0, EDGE)]
            pltpu.make_async_copy(edge, edge, hrecv.at[2 + p]).wait()

    b_at = bc_cols(me, 0)
    c_at = bc_cols(me, 1)

    @pl.loop(0, N_INNER)
    def _(j):
        slot = dtbuf.at[j]
        pltpu.make_async_copy(slot, slot, srecv.at[2, j]).wait()
        raw = dtbuf[j].astype(F32) + bias_col
        dt = jnp.maximum(raw, 0.0) + jnp.log1p(jnp.exp(-jnp.abs(raw)))
        da = dt * rate_col
        cumul = jnp.dot(da, upto, preferred_element_type=F32, precision=lax.Precision.HIGHEST)
        grow = jnp.exp(-cumul) * dt
        decay = jnp.exp(cumul)
        grow_hi = grow.astype(BF16).astype(F32)
        decay_hi = decay.astype(BF16).astype(F32)
        parts = jnp.concatenate(
            [grow_hi, grow - grow_hi, decay_hi, decay - decay_hi, jnp.zeros((4 * NH, SPAN), F32)],
            axis=0,
        )
        at = pl.ds(pl.multiple_of(j * SPAN, SPAN), SPAN)
        coef_j = parts.T.astype(BF16)
        coef[at, :] = coef_j
        dec_j = dot(coef_j[SPAN - EDGE :], ee[...])[EDGE - 1 : EDGE]
        dec[j] = dec_j
        ep[j + 1] = ep[j] * dec_j

        for k, buf in enumerate((bbuf, cbuf)):
            slot = buf.at[rows_of(j)]
            pltpu.make_async_copy(slot, slot, srecv.at[k, j]).wait()

        def conv_of(buf, cols):
            weight, bias = wbc_ref[:, cols], bbc_ref[:, cols]
            return jnp.concatenate(
                [
                    conv_silu(
                        buf[pl.ds(pl.multiple_of(j * SPAN + r, EDGE), SUB + EDGE), :], weight, bias
                    )
                    for r in range(0, SPAN, SUB)
                ],
                axis=0,
            )

        b_j = conv_of(bbuf, b_at)
        c_j = conv_of(cbuf, c_at)
        cc[at, :] = c_j
        b_t = b_j.astype(F32).T.astype(BF16)
        bt[at, :] = b_t
        gm[at, :] = jnp.where(row_ids >= col_ids, dot(c_j, b_t), 0.0).astype(BF16)

    def tot_copy(k):
        return remote(ep.at[N_INNER], tot.at[slab], tsend.at[k], trecv.at[slab], (slab + k, me))

    for k in range(1, N_SLAB):

        @pl.when(slab + k < N_SLAB)
        def _():
            tot_copy(k).start()

    @pl.loop(0, slab)
    def _(m):
        slot = tot.at[m]
        pltpu.make_async_copy(slot, slot, trecv.at[m]).wait()

    def end_copy(p, k):
        return remote(
            ebuf.at[p], arr.at[p, slab], esend.at[p, k], erecv.at[p, slab], (slab + k, me)
        )

    def out_copy(p, j):
        at = pl.ds(pl.multiple_of(j * SPAN, SPAN), SPAN)
        return pltpu.make_async_copy(
            xc.at[p % 2, at], out_ref.at[at, pl.ds(p * COLS, COLS)], osem.at[p % 2, j]
        )

    def gather_pass(p):
        par = p % 2
        lanes = slice(p * COLS, (p + 1) * COLS)
        own_cols = x_cols(me, p)
        state[par, 0] = jnp.zeros((STATE, COLS), F32)

        @pl.loop(0, N_INNER)
        def _(j):
            slot = xbuf.at[p, rows_of(j)]
            pltpu.make_async_copy(slot, slot, xrecv.at[p, j]).wait()
            weight, bias = wx_ref[:, own_cols], bx_ref[:, own_cols]
            parts = []
            for r in range(0, SPAN, SUB):
                at = pl.ds(pl.multiple_of(j * SPAN + r, SUB), SUB)
                x_r = conv_silu(
                    xbuf[p, pl.ds(pl.multiple_of(j * SPAN + r, EDGE), SUB + EDGE), :], weight, bias
                )
                xc[par, at, :] = x_r
                scaled = (x_r.astype(F32) * dot(coef[at, :], ew[:, lanes])).astype(BF16)
                xs[par, at, :] = scaled
                parts.append(scaled)
            at = pl.ds(pl.multiple_of(j * SPAN, SPAN), SPAN)
            added = dot(bt[at, :], jnp.concatenate(parts, axis=0))
            state[par, j + 1] = dec[j, :, lanes] * (state[par, j] + added)

        ebuf[p] = state[par, N_INNER].astype(BF16)
        for k in range(1, N_SLAB):

            @pl.when(slab + k < N_SLAB)
            def _():
                end_copy(p, k).start()

    def output_pass(p):
        par = p % 2
        lanes = slice(p * COLS, (p + 1) * COLS)
        inc[...] = jnp.zeros((STATE, COLS), F32)

        @pl.loop(0, slab)
        def _(m):
            slot = arr.at[p, m]
            pltpu.make_async_copy(slot, slot, erecv.at[p, m]).wait()
            inc[...] = tot[m, :, lanes] * inc[...] + arr[p, m].astype(F32)

        @pl.loop(0, N_INNER)
        def _(j):
            at = pl.ds(pl.multiple_of(j * SPAN, SPAN), SPAN)
            before = (state[par, j] + ep[j, :, lanes] * inc[...]).astype(BF16)
            acc = dot(gm[at, :], xs[par, at, :]) + dot(cc[at, :], before)
            acc = acc * dot(coef[at, :], ee[:, lanes])
            y = acc + skip[:, lanes] * xc[par, at, :].astype(F32)
            xc[par, at, :] = y.astype(BF16)
            out_copy(p, j).start()

    def out_wait(p):
        @pl.loop(0, N_INNER)
        def _(j):
            out_copy(p, j).wait()

    for p in range(PIECES + 1):
        if p < PIECES:
            if p >= 2:
                out_wait(p - 2)
            gather_pass(p)
        if p >= 1:
            output_pass(p - 1)
    out_wait(PIECES - 2)
    out_wait(PIECES - 1)

    for n in range(N_PEER):
        bc_copy(n, 0).wait_send()
        bc_copy(n, 1).wait_send()
        dt_copy(n).wait_send()
        for p in range(PIECES):
            x_copy(n, p).wait_send()

    @pl.when(halo_out)
    def _():
        @pl.loop(0, N_INNER)
        def _(d):
            for copy in halo_copies(d):
                copy.wait_send()

    for k in range(1, N_SLAB):

        @pl.when(slab + k < N_SLAB)
        def _():
            tot_copy(k).wait_send()
            for p in range(PIECES):
                end_copy(p, k).wait_send()


def shards(
    x_in, bc_in, dt_raw, dt_bias, a_log, d_skip, conv_x_weight, conv_x_bias, conv_bc_weight, conv_bc_bias
):
    tok_slab = N_INNER * SPAN
    whole = pl.BlockSpec(memory_space=pltpu.VMEM)
    anywhere = pl.BlockSpec(memory_space=pl.ANY)
    dma = pltpu.SemaphoreType.DMA
    return pl.pallas_call(
        body,
        out_shape=jax.ShapeDtypeStruct((tok_slab, CH), BF16),
        in_specs=[anywhere, anywhere] + [whole] * 6,
        out_specs=anywhere,
        scratch_shapes=[
            pltpu.VMEM((PIECES, EDGE + tok_slab, COLS), BF16),
            pltpu.VMEM((EDGE + tok_slab, STATE), BF16),
            pltpu.VMEM((EDGE + tok_slab, STATE), BF16),
            pltpu.VMEM((N_INNER, NH, SPAN), BF16),
            pltpu.VMEM((HEADS, SPAN), BF16),
            pltpu.VMEM((tok_slab, SPAN), BF16),
            pltpu.VMEM((tok_slab, STATE), BF16),
            pltpu.VMEM((tok_slab, SPAN), BF16),
            pltpu.VMEM((tok_slab, 128), BF16),
            pltpu.VMEM((128, CH), BF16),
            pltpu.VMEM((128, CH), BF16),
            pltpu.VMEM((N_INNER, 1, CH), F32),
            pltpu.VMEM((N_INNER + 1, 1, CH), F32),
            pltpu.VMEM((N_SLAB, 1, CH), F32),
            pltpu.VMEM((1, CH), F32),
            pltpu.VMEM((2, N_INNER + 1, STATE, COLS), F32),
            pltpu.VMEM((2, tok_slab, COLS), BF16),
            pltpu.VMEM((2, tok_slab, COLS), BF16),
            pltpu.VMEM((PIECES, STATE, COLS), BF16),
            pltpu.VMEM((PIECES, N_SLAB, STATE, COLS), BF16),
            pltpu.VMEM((STATE, COLS), F32),
            dma((PIECES, N_PEER)),
            dma((PIECES, N_INNER)),
            dma((3, N_PEER)),
            dma((3, N_INNER)),
            dma((2 + PIECES, N_INNER)),
            dma((2 + PIECES,)),
            dma((N_SLAB,)),
            dma((N_SLAB,)),
            dma((PIECES, N_SLAB)),
            dma((PIECES, N_SLAB)),
            dma((2, N_INNER)),
        ],
        compiler_params=pltpu.CompilerParams(
            collective_id=0, has_side_effects=True, vmem_limit_bytes=56 * 2**20
        ),
        cost_estimate=pl.CostEstimate(
            flops=9 * 10**9, bytes_accessed=18 * 2**20, transcendentals=6 * 2**20
        ),
    )(
        x_in,
        bc_in,
        dt_raw,
        jnp.stack([dt_bias, a_log, d_skip], axis=1),
        conv_x_weight,
        conv_x_bias[None, :],
        conv_bc_weight,
        conv_bc_bias[None, :],
    )


def solution(mesh):
    rows = P(("slab", "inner"), None)
    return jax.shard_map(
        shards,
        mesh=mesh,
        in_specs=(rows, rows, rows) + (P(),) * 7,
        out_specs=P("slab", "inner"),
        check_vma=False,
    )
```

```python
import jax
import jax.numpy as jnp
from jax import lax
from jax.experimental import pallas as pl
from jax.experimental.pallas import tpu as pltpu
from jax.sharding import PartitionSpec as P

HEADS = 256
HEADDIM = 64
STATE = 256
GROUPS = 8
SPAN = 256
N_SLAB = 8
N_INNER = 16
CH = 1024
NH = 16
CUTS = (0, 256, 512, 768, 896, 1024)
PIECES = len(CUTS) - 1
BC = 2 * GROUPS * STATE
C_EARLY = 8
EDGE = 16
SUB = 64
MESH = pl.DeviceIdType.MESH
ORDER = (
    (2, 2), (1, 0), (0, 3), (3, 1), (2, 1), (0, 1), (3, 0), (1, 3),
    (1, 2), (2, 0), (3, 3), (0, 2), (1, 1), (2, 3), (3, 2),
)
N_PEER = len(ORDER)
F32 = jnp.float32
BF16 = jnp.bfloat16


def dot(a, b):
    return jnp.dot(a, b, preferred_element_type=F32)


def conv_silu(rows, weight, bias):
    full = rows.astype(F32)
    n = rows.shape[0] - EDGE
    acc = bias
    for k in range(4):
        start = EDGE - 3 + k
        acc = acc + weight[k : k + 1, :] * full[start : start + n]
    half = 0.5 * acc
    return (half + half * jnp.tanh(half)).astype(BF16)


def body(
    x_ref, bc_ref, dt_ref, bias_ref, alog_ref, skip_ref, wx_ref, bx_ref, wbc_ref, bbc_ref,
    out_ref,
    xbuf, xhalo, edge, bcraw, bcconv, bbuf, cbuf, dtbuf, dt_t, heads, bt, coef, ew, ee, dec, ep, tot, skip,
    state, carry, xs, ebuf, arr, inc,
    xsend, xrecv, ssend, srecv, hsend, hrecv, bhsend, bhrecv, bsem, tsend, trecv, esend, erecv, osem,
):
    slab = lax.axis_index("slab")
    me = lax.axis_index("inner")
    my_z, my_x = me // 4, lax.rem(me, 4)
    sign = 1 - 2 * lax.rem(slab, 2)

    def at_offset(dx, dz, way):
        return lax.rem(my_z + way * dz + 4, 4) * 4 + lax.rem(my_x + way * dx + 4, 4)

    peers = [at_offset(dx, dz, sign) for dx, dz in ORDER]
    sources = [at_offset(dx, dz, -sign) for dx, dz in ORDER]
    halo_out = jnp.logical_and(me == N_INNER - 1, slab < N_SLAB - 1)
    not_first = jnp.logical_or(me > 0, slab > 0)
    not_last = jnp.logical_or(me < N_INNER - 1, slab < N_SLAB - 1)

    barrier = pltpu.get_barrier_semaphore()
    for peer in peers:
        pl.semaphore_signal(barrier, inc=1, device_id=(slab, peer), device_id_type=MESH)
    for k in range(1, N_SLAB):

        @pl.when(slab >= k)
        def _():
            pl.semaphore_signal(barrier, inc=1, device_id=(slab - k, me), device_id_type=MESH)

    @pl.when(slab > 0)
    def _():
        pl.semaphore_signal(barrier, inc=1, device_id=(slab - 1, N_INNER - 1), device_id_type=MESH)

    own_bc = pltpu.make_async_copy(bc_ref, bcraw.at[pl.ds(EDGE, SPAN)], bsem)
    own_bc.start()
    pl.semaphore_wait(
        barrier, N_PEER + (N_SLAB - 1 - slab) + jnp.where(halo_out, N_INNER, 0)
    )

    def block(j):
        return pl.ds(pl.multiple_of(j * SPAN, SPAN), SPAN)

    def lanes_of(p):
        return slice(CUTS[p], CUTS[p + 1])

    def lane_ds(p):
        return pl.ds(CUTS[p], CUTS[p + 1] - CUTS[p])

    def x_cols(d, p):
        return pl.ds(pl.multiple_of(d * CH + CUTS[p], 128), CUTS[p + 1] - CUTS[p])

    def bc_cols(d, which):
        return pl.ds(pl.multiple_of((d // 2 + which * GROUPS) * STATE, STATE), STATE)

    def head_rows(d):
        return pl.ds(pl.multiple_of(d * NH, NH), NH)

    def remote(src, dst, send_sem, recv_sem, to):
        return pltpu.make_async_remote_copy(
            src, dst, send_sem, recv_sem, device_id=to, device_id_type=MESH
        )

    def landed(ref, sem):
        pltpu.make_async_copy(ref, ref, sem).wait()

    def bc_copy(n, which):
        return remote(
            bcconv.at[:, bc_cols(peers[n], which)], (bbuf, cbuf)[which].at[block(me)],
            ssend.at[which, n], srecv.at[which, me], (slab, peers[n]),
        )

    def dt_copy(n):
        return remote(
            dt_t.at[head_rows(peers[n])], dtbuf.at[me], ssend.at[2, n], srecv.at[2, me], (slab, peers[n])
        )

    def x_copy(n, p):
        return remote(
            x_ref.at[:, x_cols(peers[n], p)], xbuf.at[block(me), lane_ds(p)],
            xsend.at[p, n], xrecv.at[p, me], (slab, peers[n]),
        )

    tail = pl.ds(SPAN - EDGE, EDGE)

    def x_halo_copy(d):
        return remote(
            x_ref.at[tail, pl.ds(pl.multiple_of(d * CH, CH), CH)], xhalo, hsend.at[d], hrecv, (slab + 1, d)
        )

    def bc_halo_copy():
        wrap = me // (N_INNER - 1)
        return remote(
            bc_ref.at[tail], bcraw.at[pl.ds(0, EDGE)], bhsend, bhrecv, (slab + wrap, (me + 1) * (1 - wrap))
        )

    @pl.when(not_last)
    def _():
        bc_halo_copy().start()

    for n in range(N_PEER):
        x_copy(n, 0).start()

    dt_t[...] = dt_ref[...].astype(F32).T.astype(BF16)
    for n in range(N_PEER):
        dt_copy(n).start()

    @pl.when(halo_out)
    def _():
        @pl.loop(0, N_INNER)
        def _(d):
            x_halo_copy(d).start()

    own_dt = pltpu.make_async_copy(dt_t.at[head_rows(me)], dtbuf.at[me], srecv.at[2, me])
    own_dt.start()
    for p in range(PIECES):
        pltpu.make_async_copy(
            x_ref.at[:, x_cols(me, p)], xbuf.at[block(me), lane_ds(p)], xrecv.at[p, me]
        ).start()

    @pl.when(not_first)
    def _():
        landed(bcraw.at[pl.ds(0, EDGE)], bhrecv)

    @pl.when(jnp.logical_not(not_first))
    def _():
        bcraw[pl.ds(0, EDGE), :] = jnp.zeros((EDGE, BC), BF16)

    own_bc.wait()

    @pl.loop(0, BC // STATE)
    def _(g):
        cols = pl.ds(pl.multiple_of(g * STATE, STATE), STATE)
        weight, bias = wbc_ref[:, cols], bbc_ref[:, cols]
        for r in range(0, SPAN, SUB):
            bcconv[pl.ds(r, SUB), cols] = conv_silu(bcraw[pl.ds(r, SUB + EDGE), cols], weight, bias)

    for which in range(2):
        pltpu.make_async_copy(
            bcconv.at[:, bc_cols(me, which)], (bbuf, cbuf)[which].at[block(me)], srecv.at[which, me]
        ).start()
    for n in range(N_PEER):
        bc_copy(n, 0).start()
    for p in range(1, PIECES):
        for n in range(N_PEER):
            x_copy(n, p).start()
    for n in range(C_EARLY):
        bc_copy(n, 1).start()

    chan = lax.broadcasted_iota(jnp.int32, (128, CH), 1) // HEADDIM
    row = lax.broadcasted_iota(jnp.int32, (128, CH), 0)
    ew[...] = jnp.where((row < 2 * NH) & (lax.rem(row, NH) == chan), 1.0, 0.0).astype(BF16)
    ee[...] = jnp.where(
        (row >= 2 * NH) & (row < 4 * NH) & (lax.rem(row, NH) == chan), 1.0, 0.0
    ).astype(BF16)
    heads[...] = jnp.concatenate(
        [bias_ref[...], -jnp.exp(alog_ref[...]), skip_ref[...], jnp.zeros((5, HEADS), F32)], axis=0
    ).T
    own_heads = heads[head_rows(me), :]
    bias_col, rate_col, skip_col = own_heads[:, 0:1], own_heads[:, 1:2], own_heads[:, 2:3]
    pick = lax.broadcasted_iota(jnp.int32, (NH, CH), 0) == (
        lax.broadcasted_iota(jnp.int32, (NH, CH), 1) // HEADDIM
    )
    skip[...] = jnp.sum(jnp.where(pick, skip_col, 0.0), axis=0, keepdims=True)
    ep[0] = jnp.ones((1, CH), F32)
    row_ids = lax.broadcasted_iota(jnp.int32, (SPAN, SPAN), 0)
    col_ids = lax.broadcasted_iota(jnp.int32, (SPAN, SPAN), 1)
    upto = jnp.where(row_ids <= col_ids, 1.0, 0.0).astype(F32)

    @pl.when(slab == 0)
    def _():
        edge[...] = jnp.zeros((EDGE, CH), BF16)

    @pl.when(slab > 0)
    def _():
        landed(xhalo, hrecv)
        edge[...] = xhalo[...]

    @pl.loop(0, N_INNER)
    def _(j):
        landed(dtbuf.at[j], srecv.at[2, j])
        raw = dtbuf[j].astype(F32) + bias_col
        dt = jnp.maximum(raw, 0.0) + jnp.log1p(jnp.exp(-jnp.abs(raw)))
        da = dt * rate_col
        cumul = jnp.dot(da, upto, preferred_element_type=F32, precision=lax.Precision.HIGHEST)
        grow = jnp.exp(-cumul) * dt
        decay = jnp.exp(cumul)
        grow_hi = grow.astype(BF16).astype(F32)
        decay_hi = decay.astype(BF16).astype(F32)
        parts = jnp.concatenate(
            [grow_hi, grow - grow_hi, decay_hi, decay - decay_hi, jnp.zeros((4 * NH, SPAN), F32)],
            axis=0,
        )
        coef_j = parts.T.astype(BF16)
        coef[block(j), :] = coef_j
        dec_j = dot(coef_j[SPAN - EDGE :], ee[...])[EDGE - 1 : EDGE]
        dec[j] = dec_j
        ep[j + 1] = ep[j] * dec_j

    def tot_copy(k):
        return remote(ep.at[N_INNER], tot.at[slab], tsend.at[k], trecv.at[slab], (slab + k, me))

    for k in range(1, N_SLAB):

        @pl.when(slab + k < N_SLAB)
        def _():
            tot_copy(k).start()

    @pl.loop(0, slab)
    def _(m):
        landed(tot.at[m], trecv.at[m])

    @pl.loop(0, N_INNER)
    def _(j):
        landed(bbuf.at[block(j)], srecv.at[0, j])
        bt[block(j), :] = bbuf[block(j), :].astype(F32).T.astype(BF16)

    def end_copy(p, k):
        return remote(
            ebuf.at[:, lane_ds(p)], arr.at[slab, :, lane_ds(p)], esend.at[p, k], erecv.at[p, slab],
            (slab + k, me),
        )

    def gather_pass(p):
        lanes = lanes_of(p)
        own_cols = x_cols(me, p)
        width = CUTS[p + 1] - CUTS[p]
        carry[:, :width] = jnp.zeros((STATE, width), F32)

        @pl.loop(0, N_INNER)
        def _(j):
            landed(xbuf.at[block(j), lane_ds(p)], xrecv.at[p, j])
            weight, bias = wx_ref[:, own_cols], bx_ref[:, own_cols]
            before = edge[:, lanes]
            edge[:, lanes] = xbuf[pl.ds(pl.multiple_of((j + 1) * SPAN - EDGE, EDGE), EDGE), lanes]
            parts = []
            for r in reversed(range(0, SPAN, SUB)):
                at = pl.ds(pl.multiple_of(j * SPAN + r, SUB), SUB)
                if r:
                    rows = xbuf[pl.ds(pl.multiple_of(j * SPAN + r - EDGE, EDGE), SUB + EDGE), lanes]
                else:
                    rows = jnp.concatenate([before, xbuf[at, lanes]], axis=0)
                x_r = conv_silu(rows, weight, bias)
                xbuf[at, lanes] = x_r
                scaled = (x_r.astype(F32) * dot(coef[at, :], ew[:, lanes])).astype(BF16)
                xs[at, lanes] = scaled
                parts.insert(0, scaled)
            added = dot(bt[block(j), :], jnp.concatenate(parts, axis=0))
            now = carry[:, :width]
            state[j, :, lanes] = now
            carry[:, :width] = dec[j, :, lanes] * (now + added)

        ebuf[:, lanes] = carry[:, :width].astype(BF16)
        for k in range(1, N_SLAB):

            @pl.when(slab + k < N_SLAB)
            def _():
                end_copy(p, k).start()

    def incoming_pass(p):
        lanes = lanes_of(p)
        inc[:, lanes] = jnp.zeros((STATE, CUTS[p + 1] - CUTS[p]), F32)

        @pl.loop(0, slab)
        def _(m):
            landed(arr.at[m, :, lane_ds(p)], erecv.at[p, m])
            inc[:, lanes] = tot[m, :, lanes] * inc[:, lanes] + arr[m, :, lanes].astype(F32)

    for p in range(PIECES):
        gather_pass(p)
        if p == PIECES - 1:
            for n in range(C_EARLY, N_PEER):
                bc_copy(n, 1).start()
        if p:
            incoming_pass(p - 1)
    incoming_pass(PIECES - 1)

    def out_copy(j):
        return pltpu.make_async_copy(xs.at[block(j)], out_ref.at[block(j)], osem.at[j])

    @pl.loop(0, N_INNER)
    def _(i):
        j = me
        for n in range(N_PEER):
            j = jnp.where(i == n + 1, sources[n], j)
        landed(cbuf.at[block(j)], srecv.at[1, j])
        c_j = cbuf[block(j), :]
        g_j = jnp.where(row_ids >= col_ids, dot(c_j, bt[block(j), :]), 0.0).astype(BF16)
        for q in range(0, CH, 256):
            lanes = slice(q, q + 256)
            before = (state[j, :, lanes] + ep[j, :, lanes] * inc[:, lanes]).astype(BF16)
            acc = dot(g_j, xs[block(j), lanes]) + dot(c_j, before)
            acc = acc * dot(coef[block(j), :], ee[:, lanes])
            y = acc + skip[:, lanes] * xbuf[block(j), lanes].astype(F32)
            xs[block(j), lanes] = y.astype(BF16)
        out_copy(j).start()

    @pl.loop(0, N_INNER)
    def _(j):
        out_copy(j).wait()

    for n in range(N_PEER):
        bc_copy(n, 0).wait_send()
        bc_copy(n, 1).wait_send()
        dt_copy(n).wait_send()
        for p in range(PIECES):
            x_copy(n, p).wait_send()

    @pl.when(halo_out)
    def _():
        @pl.loop(0, N_INNER)
        def _(d):
            x_halo_copy(d).wait_send()

    @pl.when(not_last)
    def _():
        bc_halo_copy().wait_send()

    for k in range(1, N_SLAB):

        @pl.when(slab + k < N_SLAB)
        def _():
            tot_copy(k).wait_send()
            for p in range(PIECES):
                end_copy(p, k).wait_send()


def hand_over(y_ref, out_ref, sem):
    def copy(j):
        at = pl.ds(pl.multiple_of(j * SPAN, SPAN), SPAN)
        return pltpu.make_async_copy(y_ref.at[at], out_ref.at[at], sem.at[j])

    @pl.loop(0, N_INNER)
    def _(j):
        copy(j).start()

    @pl.loop(0, N_INNER)
    def _(j):
        copy(j).wait()


def shards(
    x_in, bc_in, dt_raw, dt_bias, a_log, d_skip, conv_x_weight, conv_x_bias, conv_bc_weight, conv_bc_bias
):
    tok_slab = N_INNER * SPAN
    whole = pl.BlockSpec(memory_space=pltpu.VMEM)
    anywhere = pl.BlockSpec(memory_space=pl.ANY)
    dma = pltpu.SemaphoreType.DMA
    y = pl.pallas_call(
        body,
        out_shape=jax.ShapeDtypeStruct((tok_slab, CH), BF16),
        in_specs=[anywhere, anywhere] + [whole] * 8,
        out_specs=anywhere,
        scratch_shapes=[
            pltpu.VMEM((tok_slab, CH), BF16),
            pltpu.VMEM((EDGE, CH), BF16),
            pltpu.VMEM((EDGE, CH), BF16),
            pltpu.VMEM((EDGE + SPAN, BC), BF16),
            pltpu.VMEM((SPAN, BC), BF16),
            pltpu.VMEM((tok_slab, STATE), BF16),
            pltpu.VMEM((tok_slab, STATE), BF16),
            pltpu.VMEM((N_INNER, NH, SPAN), BF16),
            pltpu.VMEM((HEADS, SPAN), BF16),
            pltpu.VMEM((HEADS, 8), F32),
            pltpu.VMEM((tok_slab, SPAN), BF16),
            pltpu.VMEM((tok_slab, 128), BF16),
            pltpu.VMEM((128, CH), BF16),
            pltpu.VMEM((128, CH), BF16),
            pltpu.VMEM((N_INNER, 1, CH), F32),
            pltpu.VMEM((N_INNER + 1, 1, CH), F32),
            pltpu.VMEM((N_SLAB, 1, CH), F32),
            pltpu.VMEM((1, CH), F32),
            pltpu.VMEM((N_INNER, STATE, CH), F32),
            pltpu.VMEM((STATE, 256), F32),
            pltpu.VMEM((tok_slab, CH), BF16),
            pltpu.VMEM((STATE, CH), BF16),
            pltpu.VMEM((N_SLAB, STATE, CH), BF16),
            pltpu.VMEM((STATE, CH), F32),
            dma((PIECES, N_PEER)),
            dma((PIECES, N_INNER)),
            dma((3, N_PEER)),
            dma((3, N_INNER)),
            dma((N_INNER,)),
            dma,
            dma,
            dma,
            dma,
            dma((N_SLAB,)),
            dma((N_SLAB,)),
            dma((PIECES, N_SLAB)),
            dma((PIECES, N_SLAB)),
            dma((N_INNER,)),
        ],
        compiler_params=pltpu.CompilerParams(
            collective_id=0, has_side_effects=True, vmem_limit_bytes=58 * 2**20
        ),
        cost_estimate=pl.CostEstimate(
            flops=9 * 10**9, bytes_accessed=18 * 2**20, transcendentals=6 * 2**20
        ),
    )(
        x_in,
        bc_in,
        dt_raw,
        dt_bias[None, :],
        a_log[None, :],
        d_skip[None, :],
        conv_x_weight,
        conv_x_bias[None, :],
        conv_bc_weight,
        conv_bc_bias[None, :],
    )
    return pl.pallas_call(
        hand_over,
        out_shape=jax.ShapeDtypeStruct((tok_slab, CH), BF16),
        in_specs=[anywhere],
        out_specs=anywhere,
        scratch_shapes=[dma((N_INNER,))],
        compiler_params=pltpu.CompilerParams(vmem_limit_bytes=56 * 2**20),
        cost_estimate=pl.CostEstimate(flops=0, bytes_accessed=16 * 2**20, transcendentals=0),
    )(y)


def solution(mesh):
    rows = P(("slab", "inner"), None)
    return jax.shard_map(
        shards,
        mesh=mesh,
        in_specs=(rows, rows, rows) + (P(),) * 7,
        out_specs=P("slab", "inner"),
        check_vma=False,
    )
```

```python
import jax
import jax.numpy as jnp
from jax import lax
from jax.experimental import pallas as pl
from jax.experimental.pallas import tpu as pltpu
from jax.sharding import PartitionSpec as P

HEADS = 256
HEADDIM = 64
STATE = 256
GROUPS = 8
SPAN = 256
N_SLAB = 8
N_INNER = 16
CH = 1024
NH = 16
CUTS = (0, 256, 512, 768, 896, 1024)
PIECES = len(CUTS) - 1
BC = 2 * GROUPS * STATE
C_EARLY = 8
EDGE = 16
SUB = 64
MESH = pl.DeviceIdType.MESH
ORDER = (
    (2, 2), (1, 0), (0, 3), (3, 1), (2, 1), (0, 1), (3, 0), (1, 3),
    (1, 2), (2, 0), (3, 3), (0, 2), (1, 1), (2, 3), (3, 2),
)
N_PEER = len(ORDER)
F32 = jnp.float32
BF16 = jnp.bfloat16


def dot(a, b):
    return jnp.dot(a, b, preferred_element_type=F32)


def conv_silu(rows, weight, bias):
    full = rows.astype(F32)
    n = rows.shape[0] - EDGE
    acc = bias
    for k in range(4):
        start = EDGE - 3 + k
        acc = acc + weight[k : k + 1, :] * full[start : start + n]
    half = 0.5 * acc
    return (half + half * jnp.tanh(half)).astype(BF16)


def body(
    x_ref, bc_ref, dt_ref, bias_ref, alog_ref, skip_ref, wx_ref, bx_ref, wbc_ref, bbc_ref,
    out_ref,
    xbuf, xhalo, edge, bcraw, bcconv, bbuf, cbuf, dtbuf, dt_t, heads, bt, coef, ew, ee, dec, ep, tot, skip,
    state, carry, xs, ebuf, arr, inc,
    xsend, xrecv, ssend, srecv, hsend, hrecv, bhsend, bhrecv, bsem, tsend, trecv, esend, erecv, osem,
):
    slab = lax.axis_index("slab")
    me = lax.axis_index("inner")
    my_z, my_x = me // 4, lax.rem(me, 4)
    sign = 1 - 2 * lax.rem(slab, 2)

    def at_offset(dx, dz, way):
        return lax.rem(my_z + way * dz + 4, 4) * 4 + lax.rem(my_x + way * dx + 4, 4)

    peers = [at_offset(dx, dz, sign) for dx, dz in ORDER]
    sources = [at_offset(dx, dz, -sign) for dx, dz in ORDER]
    halo_out = jnp.logical_and(me == N_INNER - 1, slab < N_SLAB - 1)
    not_first = jnp.logical_or(me > 0, slab > 0)
    not_last = jnp.logical_or(me < N_INNER - 1, slab < N_SLAB - 1)

    barrier = pltpu.get_barrier_semaphore()
    for peer in peers:
        pl.semaphore_signal(barrier, inc=1, device_id=(slab, peer), device_id_type=MESH)
    for k in range(1, N_SLAB):

        @pl.when(slab >= k)
        def _():
            pl.semaphore_signal(barrier, inc=1, device_id=(slab - k, me), device_id_type=MESH)

    @pl.when(slab > 0)
    def _():
        pl.semaphore_signal(barrier, inc=1, device_id=(slab - 1, N_INNER - 1), device_id_type=MESH)

    own_bc = pltpu.make_async_copy(bc_ref, bcraw.at[pl.ds(EDGE, SPAN)], bsem)
    own_bc.start()
    pl.semaphore_wait(
        barrier, N_PEER + (N_SLAB - 1 - slab) + jnp.where(halo_out, N_INNER, 0)
    )

    def block(j):
        return pl.ds(pl.multiple_of(j * SPAN, SPAN), SPAN)

    def lanes_of(p):
        return slice(CUTS[p], CUTS[p + 1])

    def lane_ds(p):
        return pl.ds(CUTS[p], CUTS[p + 1] - CUTS[p])

    def x_cols(d, p):
        return pl.ds(pl.multiple_of(d * CH + CUTS[p], 128), CUTS[p + 1] - CUTS[p])

    def bc_cols(d, which):
        return pl.ds(pl.multiple_of((d // 2 + which * GROUPS) * STATE, STATE), STATE)

    def head_rows(d):
        return pl.ds(pl.multiple_of(d * NH, NH), NH)

    def remote(src, dst, send_sem, recv_sem, to):
        return pltpu.make_async_remote_copy(
            src, dst, send_sem, recv_sem, device_id=to, device_id_type=MESH
        )

    def landed(ref, sem):
        pltpu.make_async_copy(ref, ref, sem).wait()

    def bc_copy(n, which):
        return remote(
            bcconv.at[:, bc_cols(peers[n], which)], (bbuf, cbuf)[which].at[block(me)],
            ssend.at[which, n], srecv.at[which, me], (slab, peers[n]),
        )

    def dt_copy(n):
        return remote(
            dt_t.at[head_rows(peers[n])], dtbuf.at[me], ssend.at[2, n], srecv.at[2, me], (slab, peers[n])
        )

    def x_copy(n, p):
        return remote(
            x_ref.at[:, x_cols(peers[n], p)], xbuf.at[block(me), lane_ds(p)],
            xsend.at[p, n], xrecv.at[p, me], (slab, peers[n]),
        )

    tail = pl.ds(SPAN - EDGE, EDGE)

    def x_halo_copy(d):
        return remote(
            x_ref.at[tail, pl.ds(pl.multiple_of(d * CH, CH), CH)], xhalo, hsend.at[d], hrecv, (slab + 1, d)
        )

    def bc_halo_copy():
        wrap = me // (N_INNER - 1)
        return remote(
            bc_ref.at[tail], bcraw.at[pl.ds(0, EDGE)], bhsend, bhrecv, (slab + wrap, (me + 1) * (1 - wrap))
        )

    @pl.when(not_last)
    def _():
        bc_halo_copy().start()

    for n in range(N_PEER):
        x_copy(n, 0).start()

    dt_t[...] = dt_ref[...].astype(F32).T.astype(BF16)
    for n in range(N_PEER):
        dt_copy(n).start()

    @pl.when(halo_out)
    def _():
        @pl.loop(0, N_INNER)
        def _(d):
            x_halo_copy(d).start()

    own_dt = pltpu.make_async_copy(dt_t.at[head_rows(me)], dtbuf.at[me], srecv.at[2, me])
    own_dt.start()
    for p in range(PIECES):
        pltpu.make_async_copy(
            x_ref.at[:, x_cols(me, p)], xbuf.at[block(me), lane_ds(p)], xrecv.at[p, me]
        ).start()

    @pl.when(not_first)
    def _():
        landed(bcraw.at[pl.ds(0, EDGE)], bhrecv)

    @pl.when(jnp.logical_not(not_first))
    def _():
        bcraw[pl.ds(0, EDGE), :] = jnp.zeros((EDGE, BC), BF16)

    own_bc.wait()

    @pl.loop(0, BC // STATE)
    def _(g):
        cols = pl.ds(pl.multiple_of(g * STATE, STATE), STATE)
        weight, bias = wbc_ref[:, cols], bbc_ref[:, cols]
        for r in range(0, SPAN, SUB):
            bcconv[pl.ds(r, SUB), cols] = conv_silu(bcraw[pl.ds(r, SUB + EDGE), cols], weight, bias)

    for which in range(2):
        pltpu.make_async_copy(
            bcconv.at[:, bc_cols(me, which)], (bbuf, cbuf)[which].at[block(me)], srecv.at[which, me]
        ).start()
    for n in range(N_PEER):
        bc_copy(n, 0).start()
    for p in range(1, PIECES):
        for n in range(N_PEER):
            x_copy(n, p).start()
    for n in range(C_EARLY):
        bc_copy(n, 1).start()

    chan = lax.broadcasted_iota(jnp.int32, (128, CH), 1) // HEADDIM
    row = lax.broadcasted_iota(jnp.int32, (128, CH), 0)
    ew[...] = jnp.where((row < 2 * NH) & (lax.rem(row, NH) == chan), 1.0, 0.0).astype(BF16)
    ee[...] = jnp.where(
        (row >= 2 * NH) & (row < 4 * NH) & (lax.rem(row, NH) == chan), 1.0, 0.0
    ).astype(BF16)
    heads[...] = jnp.concatenate(
        [bias_ref[...], -jnp.exp(alog_ref[...]), skip_ref[...], jnp.zeros((5, HEADS), F32)], axis=0
    ).T
    own_heads = heads[head_rows(me), :]
    bias_col, rate_col, skip_col = own_heads[:, 0:1], own_heads[:, 1:2], own_heads[:, 2:3]
    pick = lax.broadcasted_iota(jnp.int32, (NH, CH), 0) == (
        lax.broadcasted_iota(jnp.int32, (NH, CH), 1) // HEADDIM
    )
    skip[...] = jnp.sum(jnp.where(pick, skip_col, 0.0), axis=0, keepdims=True)
    ep[0] = jnp.ones((1, CH), F32)
    row_ids = lax.broadcasted_iota(jnp.int32, (SPAN, SPAN), 0)
    col_ids = lax.broadcasted_iota(jnp.int32, (SPAN, SPAN), 1)
    upto = jnp.where(row_ids <= col_ids, 1.0, 0.0).astype(F32)

    @pl.when(slab == 0)
    def _():
        edge[...] = jnp.zeros((EDGE, CH), BF16)

    @pl.when(slab > 0)
    def _():
        landed(xhalo, hrecv)
        edge[...] = xhalo[...]

    @pl.loop(0, N_INNER)
    def _(j):
        landed(dtbuf.at[j], srecv.at[2, j])
        raw = dtbuf[j].astype(F32) + bias_col
        dt = jnp.maximum(raw, 0.0) + jnp.log1p(jnp.exp(-jnp.abs(raw)))
        da = dt * rate_col
        cumul = jnp.dot(da, upto, preferred_element_type=F32, precision=lax.Precision.HIGHEST)
        grow = jnp.exp(-cumul) * dt
        decay = jnp.exp(cumul)
        grow_hi = grow.astype(BF16).astype(F32)
        decay_hi = decay.astype(BF16).astype(F32)
        parts = jnp.concatenate(
            [grow_hi, grow - grow_hi, decay_hi, decay - decay_hi, jnp.zeros((4 * NH, SPAN), F32)],
            axis=0,
        )
        coef_j = parts.T.astype(BF16)
        coef[block(j), :] = coef_j
        dec_j = dot(coef_j[SPAN - EDGE :], ee[...])[EDGE - 1 : EDGE]
        dec[j] = dec_j
        ep[j + 1] = ep[j] * dec_j

    def tot_copy(k):
        return remote(ep.at[N_INNER], tot.at[slab], tsend.at[k], trecv.at[slab], (slab + k, me))

    for k in range(1, N_SLAB):

        @pl.when(slab + k < N_SLAB)
        def _():
            tot_copy(k).start()

    @pl.loop(0, slab)
    def _(m):
        landed(tot.at[m], trecv.at[m])

    @pl.loop(0, N_INNER)
    def _(j):
        landed(bbuf.at[block(j)], srecv.at[0, j])
        bt[block(j), :] = bbuf[block(j), :].astype(F32).T.astype(BF16)

    def end_copy(p, k):
        return remote(
            ebuf.at[:, lane_ds(p)], arr.at[slab, :, lane_ds(p)], esend.at[p, k], erecv.at[p, slab],
            (slab + k, me),
        )

    def gather_pass(p):
        lanes = lanes_of(p)
        own_cols = x_cols(me, p)
        width = CUTS[p + 1] - CUTS[p]
        carry[:, :width] = jnp.zeros((STATE, width), F32)

        @pl.loop(0, N_INNER)
        def _(j):
            landed(xbuf.at[block(j), lane_ds(p)], xrecv.at[p, j])
            weight, bias = wx_ref[:, own_cols], bx_ref[:, own_cols]
            before = edge[:, lanes]
            edge[:, lanes] = xbuf[pl.ds(pl.multiple_of((j + 1) * SPAN - EDGE, EDGE), EDGE), lanes]
            parts = []
            for r in reversed(range(0, SPAN, SUB)):
                at = pl.ds(pl.multiple_of(j * SPAN + r, SUB), SUB)
                if r:
                    rows = xbuf[pl.ds(pl.multiple_of(j * SPAN + r - EDGE, EDGE), SUB + EDGE), lanes]
                else:
                    rows = jnp.concatenate([before, xbuf[at, lanes]], axis=0)
                x_r = conv_silu(rows, weight, bias)
                xbuf[at, lanes] = x_r
                scaled = (x_r.astype(F32) * dot(coef[at, :], ew[:, lanes])).astype(BF16)
                xs[at, lanes] = scaled
                parts.insert(0, scaled)
            added = dot(bt[block(j), :], jnp.concatenate(parts, axis=0))
            now = carry[:, :width]
            state[j, :, lanes] = now
            carry[:, :width] = dec[j, :, lanes] * (now + added)

        ebuf[:, lanes] = carry[:, :width].astype(BF16)
        for k in range(1, N_SLAB):

            @pl.when(slab + k < N_SLAB)
            def _():
                end_copy(p, k).start()

    def incoming_pass(p):
        lanes = lanes_of(p)
        inc[:, lanes] = jnp.zeros((STATE, CUTS[p + 1] - CUTS[p]), F32)

        @pl.loop(0, slab)
        def _(m):
            landed(arr.at[m, :, lane_ds(p)], erecv.at[p, m])
            inc[:, lanes] = tot[m, :, lanes] * inc[:, lanes] + arr[m, :, lanes].astype(F32)

    for p in range(PIECES):
        gather_pass(p)
        if p == PIECES - 1:
            for n in range(C_EARLY, N_PEER):
                bc_copy(n, 1).start()
        if p:
            incoming_pass(p - 1)
    incoming_pass(PIECES - 1)

    def out_copy(j):
        return pltpu.make_async_copy(xs.at[block(j)], out_ref.at[block(j)], osem.at[j])

    @pl.loop(0, N_INNER)
    def _(i):
        j = me
        for n in range(N_PEER):
            j = jnp.where(i == n + 1, sources[n], j)
        landed(cbuf.at[block(j)], srecv.at[1, j])
        c_j = cbuf[block(j), :]
        g_j = jnp.where(row_ids >= col_ids, dot(c_j, bt[block(j), :]), 0.0).astype(BF16)
        for q in range(0, CH, 256):
            lanes = slice(q, q + 256)
            before = (state[j, :, lanes] + ep[j, :, lanes] * inc[:, lanes]).astype(BF16)
            acc = dot(g_j, xs[block(j), lanes]) + dot(c_j, before)
            acc = acc * dot(coef[block(j), :], ee[:, lanes])
            y = acc + skip[:, lanes] * xbuf[block(j), lanes].astype(F32)
            xs[block(j), lanes] = y.astype(BF16)
        out_copy(j).start()

    @pl.loop(0, N_INNER)
    def _(j):
        out_copy(j).wait()

    for n in range(N_PEER):
        bc_copy(n, 0).wait_send()
        bc_copy(n, 1).wait_send()
        dt_copy(n).wait_send()
        for p in range(PIECES):
            x_copy(n, p).wait_send()

    @pl.when(halo_out)
    def _():
        @pl.loop(0, N_INNER)
        def _(d):
            x_halo_copy(d).wait_send()

    @pl.when(not_last)
    def _():
        bc_halo_copy().wait_send()

    for k in range(1, N_SLAB):

        @pl.when(slab + k < N_SLAB)
        def _():
            tot_copy(k).wait_send()
            for p in range(PIECES):
                end_copy(p, k).wait_send()


def hand_over(y_ref, out_ref, buf, isem, osem):
    def at(j):
        return pl.ds(pl.multiple_of(j * SPAN, SPAN), SPAN)

    def read(j):
        return pltpu.make_async_copy(y_ref.at[at(j)], buf.at[at(j)], isem.at[j])

    def write(j):
        return pltpu.make_async_copy(buf.at[at(j)], out_ref.at[at(j)], osem.at[j])

    @pl.loop(0, N_INNER)
    def _(j):
        read(j).start()

    @pl.loop(0, N_INNER)
    def _(j):
        read(j).wait()
        write(j).start()

    @pl.loop(0, N_INNER)
    def _(j):
        write(j).wait()


def shards(
    x_in, bc_in, dt_raw, dt_bias, a_log, d_skip, conv_x_weight, conv_x_bias, conv_bc_weight, conv_bc_bias
):
    tok_slab = N_INNER * SPAN
    whole = pl.BlockSpec(memory_space=pltpu.VMEM)
    anywhere = pl.BlockSpec(memory_space=pl.ANY)
    dma = pltpu.SemaphoreType.DMA
    y = pl.pallas_call(
        body,
        out_shape=jax.ShapeDtypeStruct((tok_slab, CH), BF16),
        in_specs=[anywhere, anywhere] + [whole] * 8,
        out_specs=anywhere,
        scratch_shapes=[
            pltpu.VMEM((tok_slab, CH), BF16),
            pltpu.VMEM((EDGE, CH), BF16),
            pltpu.VMEM((EDGE, CH), BF16),
            pltpu.VMEM((EDGE + SPAN, BC), BF16),
            pltpu.VMEM((SPAN, BC), BF16),
            pltpu.VMEM((tok_slab, STATE), BF16),
            pltpu.VMEM((tok_slab, STATE), BF16),
            pltpu.VMEM((N_INNER, NH, SPAN), BF16),
            pltpu.VMEM((HEADS, SPAN), BF16),
            pltpu.VMEM((HEADS, 8), F32),
            pltpu.VMEM((tok_slab, SPAN), BF16),
            pltpu.VMEM((tok_slab, 128), BF16),
            pltpu.VMEM((128, CH), BF16),
            pltpu.VMEM((128, CH), BF16),
            pltpu.VMEM((N_INNER, 1, CH), F32),
            pltpu.VMEM((N_INNER + 1, 1, CH), F32),
            pltpu.VMEM((N_SLAB, 1, CH), F32),
            pltpu.VMEM((1, CH), F32),
            pltpu.VMEM((N_INNER, STATE, CH), F32),
            pltpu.VMEM((STATE, 256), F32),
            pltpu.VMEM((tok_slab, CH), BF16),
            pltpu.VMEM((STATE, CH), BF16),
            pltpu.VMEM((N_SLAB, STATE, CH), BF16),
            pltpu.VMEM((STATE, CH), F32),
            dma((PIECES, N_PEER)),
            dma((PIECES, N_INNER)),
            dma((3, N_PEER)),
            dma((3, N_INNER)),
            dma((N_INNER,)),
            dma,
            dma,
            dma,
            dma,
            dma((N_SLAB,)),
            dma((N_SLAB,)),
            dma((PIECES, N_SLAB)),
            dma((PIECES, N_SLAB)),
            dma((N_INNER,)),
        ],
        compiler_params=pltpu.CompilerParams(
            collective_id=0, has_side_effects=True, vmem_limit_bytes=58 * 2**20
        ),
        cost_estimate=pl.CostEstimate(
            flops=9 * 10**9, bytes_accessed=18 * 2**20, transcendentals=6 * 2**20
        ),
    )(
        x_in,
        bc_in,
        dt_raw,
        dt_bias[None, :],
        a_log[None, :],
        d_skip[None, :],
        conv_x_weight,
        conv_x_bias[None, :],
        conv_bc_weight,
        conv_bc_bias[None, :],
    )
    return pl.pallas_call(
        hand_over,
        out_shape=jax.ShapeDtypeStruct((tok_slab, CH), BF16),
        in_specs=[anywhere],
        out_specs=anywhere,
        scratch_shapes=[pltpu.VMEM((tok_slab, CH), BF16), dma((N_INNER,)), dma((N_INNER,))],
        compiler_params=pltpu.CompilerParams(vmem_limit_bytes=56 * 2**20),
        cost_estimate=pl.CostEstimate(flops=0, bytes_accessed=16 * 2**20, transcendentals=0),
    )(y)


def solution(mesh):
    rows = P(("slab", "inner"), None)
    return jax.shard_map(
        shards,
        mesh=mesh,
        in_specs=(rows, rows, rows) + (P(),) * 7,
        out_specs=P("slab", "inner"),
        check_vma=False,
    )
```

```python
import jax
import jax.numpy as jnp
from jax import lax
from jax.experimental import pallas as pl
from jax.experimental.pallas import tpu as pltpu
from jax.sharding import PartitionSpec as P

HEADS = 256
HEADDIM = 64
STATE = 256
GROUPS = 8
SPAN = 256
N_SLAB = 8
N_INNER = 16
CH = 1024
NH = 16
CUTS = (0, 256, 512, 768, 896, 1024)
PIECES = len(CUTS) - 1
BC = 2 * GROUPS * STATE
C_EARLY = 11
EDGE = 16
SUB = 64
MESH = pl.DeviceIdType.MESH
ORDER = (
    (2, 2), (1, 0), (0, 3), (3, 1), (2, 1), (0, 1), (3, 0), (1, 3),
    (1, 2), (2, 0), (3, 3), (0, 2), (1, 1), (2, 3), (3, 2),
)
N_PEER = len(ORDER)
F32 = jnp.float32
BF16 = jnp.bfloat16


def dot(a, b):
    return jnp.dot(a, b, preferred_element_type=F32)


def conv_silu(rows, weight, bias):
    full = rows.astype(F32)
    n = rows.shape[0] - EDGE
    acc = bias
    for k in range(4):
        start = EDGE - 3 + k
        acc = acc + weight[k : k + 1, :] * full[start : start + n]
    half = 0.5 * acc
    return (half + half * jnp.tanh(half)).astype(BF16)


def body(
    x_ref, bc_ref, dt_ref, bias_ref, alog_ref, skip_ref, wx_ref, bx_ref, wbc_ref, bbc_ref,
    out_ref,
    xbuf, xlast, xpack, xhalo, edge, bcraw, bctail, bchalo, bcconv, bbuf, cbuf, dtbuf, dt_t, heads, bt, coef, ew, ee, dec, ep, tot, skip,
    state, carry, xs, ebuf, arr, inc,
    xsend, xrecv, ssend, srecv, hsend, hrecv, bhsend, bhrecv, bsem, lsem, tsend, trecv, esend, erecv, osem,
):
    slab = lax.axis_index("slab")
    me = lax.axis_index("inner")
    my_z, my_x = me // 4, lax.rem(me, 4)
    sign = 1 - 2 * lax.rem(slab, 2)

    def at_offset(dx, dz, way):
        return lax.rem(my_z + way * dz + 4, 4) * 4 + lax.rem(my_x + way * dx + 4, 4)

    peers = [at_offset(dx, dz, sign) for dx, dz in ORDER]
    sources = [at_offset(dx, dz, -sign) for dx, dz in ORDER]
    not_first = jnp.logical_or(me > 0, slab > 0)
    not_last = jnp.logical_or(me < N_INNER - 1, slab < N_SLAB - 1)

    barrier = pltpu.get_barrier_semaphore()
    for peer in peers:
        pl.semaphore_signal(barrier, inc=1, device_id=(slab, peer), device_id_type=MESH)
    for k in range(1, N_SLAB):

        @pl.when(slab >= k)
        def _():
            pl.semaphore_signal(barrier, inc=1, device_id=(slab - k, me), device_id_type=MESH)

    @pl.when(slab > 0)
    def _():
        pl.semaphore_signal(barrier, inc=1, device_id=(slab - 1, N_INNER - 1), device_id_type=MESH)

    own_bc = pltpu.make_async_copy(bc_ref, bcraw.at[pl.ds(EDGE, SPAN)], bsem)
    own_bc.start()
    halo_out = jnp.logical_and(me == N_INNER - 1, slab < N_SLAB - 1)
    own_last = pltpu.make_async_copy(x_ref.at[pl.ds(SPAN - EDGE, EDGE)], xlast, lsem)

    @pl.when(halo_out)
    def _():
        own_last.start()

    pl.semaphore_wait(
        barrier, N_PEER + (N_SLAB - 1 - slab) + jnp.where(halo_out, N_INNER, 0)
    )

    def block(j):
        return pl.ds(pl.multiple_of(j * SPAN, SPAN), SPAN)

    def lanes_of(p):
        return slice(CUTS[p], CUTS[p + 1])

    def lane_ds(p):
        return pl.ds(CUTS[p], CUTS[p + 1] - CUTS[p])

    def x_cols(d, p):
        return pl.ds(pl.multiple_of(d * CH + CUTS[p], 128), CUTS[p + 1] - CUTS[p])

    def bc_cols(d, which):
        return pl.ds(pl.multiple_of((d // 2 + which * GROUPS) * STATE, STATE), STATE)

    def head_rows(d):
        return pl.ds(pl.multiple_of(d * NH, NH), NH)

    def remote(src, dst, send_sem, recv_sem, to):
        return pltpu.make_async_remote_copy(
            src, dst, send_sem, recv_sem, device_id=to, device_id_type=MESH
        )

    def landed(ref, sem):
        pltpu.make_async_copy(ref, ref, sem).wait()

    def bc_copy(n, which):
        return remote(
            bcconv.at[:, bc_cols(peers[n], which)], (bbuf, cbuf)[which].at[block(me)],
            ssend.at[which, n], srecv.at[which, me], (slab, peers[n]),
        )

    def dt_copy(n):
        return remote(
            dt_t.at[head_rows(peers[n])], dtbuf.at[me], ssend.at[2, n], srecv.at[2, me], (slab, peers[n])
        )

    def x_copy(n, p):
        return remote(
            x_ref.at[:, x_cols(peers[n], p)], xbuf.at[block(me), lane_ds(p)],
            xsend.at[p, n], xrecv.at[p, me], (slab, peers[n]),
        )

    def x_halo_copy(d):
        return remote(xpack.at[d], xhalo, hsend.at[d], hrecv, (slab + 1, d))

    def bc_halo_copy():
        wrap = me // (N_INNER - 1)
        return remote(bctail, bchalo, bhsend, bhrecv, (slab + wrap, (me + 1) * (1 - wrap)))

    def pack(rows, width):
        last = rows.astype(F32)[EDGE - 3 :]
        groups = rows.shape[1] // width
        return jnp.concatenate(
            [last[:, q * width : (q + 1) * width] for q in range(groups)]
            + [jnp.zeros((EDGE - 3 * groups, width), F32)],
            axis=0,
        ).astype(BF16)

    def unpack(packed, q):
        return jnp.concatenate(
            [jnp.zeros((EDGE - 3, packed.shape[1]), F32), packed.astype(F32)[3 * q : 3 * q + 3]], axis=0
        ).astype(BF16)

    own_bc.wait()
    bctail[...] = pack(bcraw[pl.ds(SPAN, EDGE), :], CH)

    @pl.when(not_last)
    def _():
        bc_halo_copy().start()

    for n in range(N_PEER):
        x_copy(n, 0).start()

    @pl.when(halo_out)
    def _():
        own_last.wait()

        @pl.loop(0, N_INNER)
        def _(d):
            xpack[d] = pack(xlast[:, pl.ds(pl.multiple_of(d * CH, CH), CH)], 256)
            x_halo_copy(d).start()

    dt_t[...] = dt_ref[...].astype(F32).T.astype(BF16)
    for n in range(N_PEER):
        dt_copy(n).start()

    own_dt = pltpu.make_async_copy(dt_t.at[head_rows(me)], dtbuf.at[me], srecv.at[2, me])
    own_dt.start()
    for p in range(PIECES):
        pltpu.make_async_copy(
            x_ref.at[:, x_cols(me, p)], xbuf.at[block(me), lane_ds(p)], xrecv.at[p, me]
        ).start()

    @pl.when(not_first)
    def _():
        landed(bchalo, bhrecv)
        for q in range(BC // CH):
            bcraw[pl.ds(0, EDGE), q * CH : (q + 1) * CH] = unpack(bchalo[...], q)

    @pl.when(jnp.logical_not(not_first))
    def _():
        bcraw[pl.ds(0, EDGE), :] = jnp.zeros((EDGE, BC), BF16)

    @pl.loop(0, BC // STATE)
    def _(g):
        cols = pl.ds(pl.multiple_of(g * STATE, STATE), STATE)
        weight, bias = wbc_ref[:, cols], bbc_ref[:, cols]
        for r in range(0, SPAN, SUB):
            bcconv[pl.ds(r, SUB), cols] = conv_silu(bcraw[pl.ds(r, SUB + EDGE), cols], weight, bias)

    for which in range(2):
        pltpu.make_async_copy(
            bcconv.at[:, bc_cols(me, which)], (bbuf, cbuf)[which].at[block(me)], srecv.at[which, me]
        ).start()
    for n in range(N_PEER):
        bc_copy(n, 0).start()
    for n in range(N_PEER):
        x_copy(n, 1).start()

    chan = lax.broadcasted_iota(jnp.int32, (128, CH), 1) // HEADDIM
    row = lax.broadcasted_iota(jnp.int32, (128, CH), 0)
    ew[...] = jnp.where((row < 2 * NH) & (lax.rem(row, NH) == chan), 1.0, 0.0).astype(BF16)
    ee[...] = jnp.where(
        (row >= 2 * NH) & (row < 4 * NH) & (lax.rem(row, NH) == chan), 1.0, 0.0
    ).astype(BF16)
    heads[...] = jnp.concatenate(
        [bias_ref[...], -jnp.exp(alog_ref[...]), skip_ref[...], jnp.zeros((5, HEADS), F32)], axis=0
    ).T
    own_heads = heads[head_rows(me), :]
    bias_col, rate_col, skip_col = own_heads[:, 0:1], own_heads[:, 1:2], own_heads[:, 2:3]
    pick = lax.broadcasted_iota(jnp.int32, (NH, CH), 0) == (
        lax.broadcasted_iota(jnp.int32, (NH, CH), 1) // HEADDIM
    )
    skip[...] = jnp.sum(jnp.where(pick, skip_col, 0.0), axis=0, keepdims=True)
    ep[0] = jnp.ones((1, CH), F32)
    row_ids = lax.broadcasted_iota(jnp.int32, (SPAN, SPAN), 0)
    col_ids = lax.broadcasted_iota(jnp.int32, (SPAN, SPAN), 1)
    upto = jnp.where(row_ids <= col_ids, 1.0, 0.0).astype(F32)

    @pl.loop(0, N_INNER)
    def _(j):
        landed(dtbuf.at[j], srecv.at[2, j])
        raw = dtbuf[j].astype(F32) + bias_col
        dt = jnp.maximum(raw, 0.0) + jnp.log1p(jnp.exp(-jnp.abs(raw)))
        da = dt * rate_col
        cumul = jnp.dot(da, upto, preferred_element_type=F32, precision=lax.Precision.HIGHEST)
        grow = jnp.exp(-cumul) * dt
        decay = jnp.exp(cumul)
        grow_hi = grow.astype(BF16).astype(F32)
        decay_hi = decay.astype(BF16).astype(F32)
        parts = jnp.concatenate(
            [grow_hi, grow - grow_hi, decay_hi, decay - decay_hi, jnp.zeros((4 * NH, SPAN), F32)],
            axis=0,
        )
        coef_j = parts.T.astype(BF16)
        coef[block(j), :] = coef_j
        dec_j = dot(coef_j[SPAN - EDGE :], ee[...])[EDGE - 1 : EDGE]
        dec[j] = dec_j
        ep[j + 1] = ep[j] * dec_j

    def tot_copy(k):
        return remote(ep.at[N_INNER], tot.at[slab], tsend.at[k], trecv.at[slab], (slab + k, me))

    for k in range(1, N_SLAB):

        @pl.when(slab + k < N_SLAB)
        def _():
            tot_copy(k).start()

    @pl.loop(0, slab)
    def _(m):
        landed(tot.at[m], trecv.at[m])

    @pl.loop(0, N_INNER)
    def _(j):
        landed(bbuf.at[block(j)], srecv.at[0, j])
        bt[block(j), :] = bbuf[block(j), :].astype(F32).T.astype(BF16)

    def end_copy(p, k):
        return remote(
            ebuf.at[:, lane_ds(p)], arr.at[slab, :, lane_ds(p)], esend.at[p, k], erecv.at[p, slab],
            (slab + k, me),
        )

    def gather_pass(p):
        lanes = lanes_of(p)
        own_cols = x_cols(me, p)
        width = CUTS[p + 1] - CUTS[p]
        carry[:, :width] = jnp.zeros((STATE, width), F32)

        if p == 0:

            @pl.when(slab > 0)
            def _():
                landed(xhalo, hrecv)
                for q in range(CH // 256):
                    edge[:, q * 256 : (q + 1) * 256] = unpack(xhalo[...], q)

            @pl.when(slab == 0)
            def _():
                edge[...] = jnp.zeros((EDGE, CH), BF16)

        @pl.loop(0, N_INNER)
        def _(j):
            landed(xbuf.at[block(j), lane_ds(p)], xrecv.at[p, j])
            weight, bias = wx_ref[:, own_cols], bx_ref[:, own_cols]
            before = edge[:, lanes]
            edge[:, lanes] = xbuf[pl.ds(pl.multiple_of((j + 1) * SPAN - EDGE, EDGE), EDGE), lanes]
            parts = []
            for r in reversed(range(0, SPAN, SUB)):
                at = pl.ds(pl.multiple_of(j * SPAN + r, SUB), SUB)
                if r:
                    rows = xbuf[pl.ds(pl.multiple_of(j * SPAN + r - EDGE, EDGE), SUB + EDGE), lanes]
                else:
                    rows = jnp.concatenate([before, xbuf[at, lanes]], axis=0)
                x_r = conv_silu(rows, weight, bias)
                xbuf[at, lanes] = x_r
                scaled = (x_r.astype(F32) * dot(coef[at, :], ew[:, lanes])).astype(BF16)
                xs[at, lanes] = scaled
                parts.insert(0, scaled)
            added = dot(bt[block(j), :], jnp.concatenate(parts, axis=0))
            now = carry[:, :width]
            state[j, :, lanes] = now
            carry[:, :width] = dec[j, :, lanes] * (now + added)

        ebuf[:, lanes] = carry[:, :width].astype(BF16)
        for k in range(1, N_SLAB):

            @pl.when(slab + k < N_SLAB)
            def _():
                end_copy(p, k).start()

    def incoming_pass(p):
        lanes = lanes_of(p)
        inc[:, lanes] = jnp.zeros((STATE, CUTS[p + 1] - CUTS[p]), F32)

        @pl.loop(0, slab)
        def _(m):
            landed(arr.at[m, :, lane_ds(p)], erecv.at[p, m])
            inc[:, lanes] = tot[m, :, lanes] * inc[:, lanes] + arr[m, :, lanes].astype(F32)

    for p in range(PIECES):
        gather_pass(p)
        if p + 2 < PIECES:
            for n in range(N_PEER):
                x_copy(n, p + 2).start()
        if p == PIECES - 2:
            for n in range(C_EARLY):
                bc_copy(n, 1).start()
        if p == PIECES - 1:
            for n in range(C_EARLY, N_PEER):
                bc_copy(n, 1).start()
        if p:
            incoming_pass(p - 1)
    incoming_pass(PIECES - 1)

    def out_copy(j):
        return pltpu.make_async_copy(xs.at[block(j)], out_ref.at[block(j)], osem.at[j])

    @pl.loop(0, N_INNER)
    def _(i):
        j = me
        for n in range(N_PEER):
            j = jnp.where(i == n + 1, sources[n], j)
        landed(cbuf.at[block(j)], srecv.at[1, j])
        c_j = cbuf[block(j), :]
        g_j = jnp.where(row_ids >= col_ids, dot(c_j, bt[block(j), :]), 0.0).astype(BF16)
        for q in range(0, CH, 256):
            lanes = slice(q, q + 256)
            before = (state[j, :, lanes] + ep[j, :, lanes] * inc[:, lanes]).astype(BF16)
            acc = dot(g_j, xs[block(j), lanes]) + dot(c_j, before)
            acc = acc * dot(coef[block(j), :], ee[:, lanes])
            y = acc + skip[:, lanes] * xbuf[block(j), lanes].astype(F32)
            xs[block(j), lanes] = y.astype(BF16)
        out_copy(j).start()

    @pl.loop(0, N_INNER)
    def _(j):
        out_copy(j).wait()

    for n in range(N_PEER):
        bc_copy(n, 0).wait_send()
        bc_copy(n, 1).wait_send()
        dt_copy(n).wait_send()
        for p in range(PIECES):
            x_copy(n, p).wait_send()

    @pl.when(halo_out)
    def _():
        @pl.loop(0, N_INNER)
        def _(d):
            x_halo_copy(d).wait_send()

    @pl.when(not_last)
    def _():
        bc_halo_copy().wait_send()

    for k in range(1, N_SLAB):

        @pl.when(slab + k < N_SLAB)
        def _():
            tot_copy(k).wait_send()
            for p in range(PIECES):
                end_copy(p, k).wait_send()


def hand_over(y_ref, out_ref, buf, isem, osem):
    def at(j):
        return pl.ds(pl.multiple_of(j * SPAN, SPAN), SPAN)

    def read(j):
        return pltpu.make_async_copy(y_ref.at[at(j)], buf.at[at(j)], isem.at[j])

    def write(j):
        return pltpu.make_async_copy(buf.at[at(j)], out_ref.at[at(j)], osem.at[j])

    @pl.loop(0, N_INNER)
    def _(j):
        read(j).start()

    @pl.loop(0, N_INNER)
    def _(j):
        read(j).wait()
        write(j).start()

    @pl.loop(0, N_INNER)
    def _(j):
        write(j).wait()


def shards(
    x_in, bc_in, dt_raw, dt_bias, a_log, d_skip, conv_x_weight, conv_x_bias, conv_bc_weight, conv_bc_bias
):
    tok_slab = N_INNER * SPAN
    whole = pl.BlockSpec(memory_space=pltpu.VMEM)
    anywhere = pl.BlockSpec(memory_space=pl.ANY)
    dma = pltpu.SemaphoreType.DMA
    y = pl.pallas_call(
        body,
        out_shape=jax.ShapeDtypeStruct((tok_slab, CH), BF16),
        in_specs=[anywhere, anywhere] + [whole] * 8,
        out_specs=anywhere,
        scratch_shapes=[
            pltpu.VMEM((tok_slab, CH), BF16),
            pltpu.VMEM((EDGE, N_INNER * CH), BF16),
            pltpu.VMEM((N_INNER, EDGE, 256), BF16),
            pltpu.VMEM((EDGE, 256), BF16),
            pltpu.VMEM((EDGE, CH), BF16),
            pltpu.VMEM((EDGE + SPAN, BC), BF16),
            pltpu.VMEM((EDGE, CH), BF16),
            pltpu.VMEM((EDGE, CH), BF16),
            pltpu.VMEM((SPAN, BC), BF16),
            pltpu.VMEM((tok_slab, STATE), BF16),
            pltpu.VMEM((tok_slab, STATE), BF16),
            pltpu.VMEM((N_INNER, NH, SPAN), BF16),
            pltpu.VMEM((HEADS, SPAN), BF16),
            pltpu.VMEM((HEADS, 8), F32),
            pltpu.VMEM((tok_slab, SPAN), BF16),
            pltpu.VMEM((tok_slab, 128), BF16),
            pltpu.VMEM((128, CH), BF16),
            pltpu.VMEM((128, CH), BF16),
            pltpu.VMEM((N_INNER, 1, CH), F32),
            pltpu.VMEM((N_INNER + 1, 1, CH), F32),
            pltpu.VMEM((N_SLAB, 1, CH), F32),
            pltpu.VMEM((1, CH), F32),
            pltpu.VMEM((N_INNER, STATE, CH), F32),
            pltpu.VMEM((STATE, 256), F32),
            pltpu.VMEM((tok_slab, CH), BF16),
            pltpu.VMEM((STATE, CH), BF16),
            pltpu.VMEM((N_SLAB, STATE, CH), BF16),
            pltpu.VMEM((STATE, CH), F32),
            dma((PIECES, N_PEER)),
            dma((PIECES, N_INNER)),
            dma((3, N_PEER)),
            dma((3, N_INNER)),
            dma((N_INNER,)),
            dma,
            dma,
            dma,
            dma,
            dma,
            dma((N_SLAB,)),
            dma((N_SLAB,)),
            dma((PIECES, N_SLAB)),
            dma((PIECES, N_SLAB)),
            dma((N_INNER,)),
        ],
        compiler_params=pltpu.CompilerParams(
            collective_id=0, has_side_effects=True, vmem_limit_bytes=58 * 2**20
        ),
        cost_estimate=pl.CostEstimate(
            flops=9 * 10**9, bytes_accessed=18 * 2**20, transcendentals=6 * 2**20
        ),
    )(
        x_in,
        bc_in,
        dt_raw,
        dt_bias[None, :],
        a_log[None, :],
        d_skip[None, :],
        conv_x_weight,
        conv_x_bias[None, :],
        conv_bc_weight,
        conv_bc_bias[None, :],
    )
    return pl.pallas_call(
        hand_over,
        out_shape=jax.ShapeDtypeStruct((tok_slab, CH), BF16),
        in_specs=[anywhere],
        out_specs=anywhere,
        scratch_shapes=[pltpu.VMEM((tok_slab, CH), BF16), dma((N_INNER,)), dma((N_INNER,))],
        compiler_params=pltpu.CompilerParams(vmem_limit_bytes=56 * 2**20),
        cost_estimate=pl.CostEstimate(flops=0, bytes_accessed=16 * 2**20, transcendentals=0),
    )(y)


def solution(mesh):
    rows = P(("slab", "inner"), None)
    return jax.shard_map(
        shards,
        mesh=mesh,
        in_specs=(rows, rows, rows) + (P(),) * 7,
        out_specs=P("slab", "inner"),
        check_vma=False,
    )
```

```python
import jax
import jax.numpy as jnp
from jax import lax
from jax.experimental import pallas as pl
from jax.experimental.pallas import tpu as pltpu
from jax.sharding import PartitionSpec as P

HEADS = 256
HEADDIM = 64
STATE = 256
GROUPS = 8
SPAN = 256
N_SLAB = 8
N_INNER = 16
CH = 1024
NH = 16
CUTS = (0, 256, 512, 768, 896, 1024)
PIECES = len(CUTS) - 1
BC = 2 * GROUPS * STATE
C_EARLY = 8
EDGE = 16
PART = 512
N_PART = 8
SUB = 64
MESH = pl.DeviceIdType.MESH
ORDER = (
    (2, 2), (1, 0), (0, 3), (3, 1), (2, 1), (0, 1), (3, 0), (1, 3),
    (1, 2), (2, 0), (3, 3), (0, 2), (1, 1), (2, 3), (3, 2),
)
N_PEER = len(ORDER)
F32 = jnp.float32
BF16 = jnp.bfloat16


def dot(a, b):
    return jnp.dot(a, b, preferred_element_type=F32)


def conv_silu(rows, weight, bias):
    full = rows.astype(F32)
    n = rows.shape[0] - EDGE
    acc = bias
    for k in range(4):
        start = EDGE - 3 + k
        acc = acc + weight[k : k + 1, :] * full[start : start + n]
    half = 0.5 * acc
    return (half + half * jnp.tanh(half)).astype(BF16)


def body(
    x_ref, bc_ref, dt_in, bias_in, alog_in, skip_in, wx_in, bx_in, wbc_in, bbc_in,
    out_ref,
    dt_ref, bias_ref, alog_ref, skip_ref, wx_ref, bx_ref, wbc_ref, bbc_ref, psem,
    xbuf, xlast, xpack, xhalo, edge, bcraw, bctail, bchalo, bcconv, bbuf, cbuf, dtbuf, dt_t, heads, bt, coef, ew, ee, dec, ep, tot, skip,
    state, carry, xs, ebuf, arr, inc,
    xsend, xrecv, ssend, srecv, hsend, hrecv, bhsend, bhrecv, bsem, lsem, tsend, trecv, esend, erecv, osem,
):
    slab = lax.axis_index("slab")
    me = lax.axis_index("inner")
    my_z, my_x = me // 4, lax.rem(me, 4)
    sign = 1 - 2 * lax.rem(slab, 2)

    def at_offset(dx, dz, way):
        return lax.rem(my_z + way * dz + 4, 4) * 4 + lax.rem(my_x + way * dx + 4, 4)

    peers = [at_offset(dx, dz, sign) for dx, dz in ORDER]
    sources = [at_offset(dx, dz, -sign) for dx, dz in ORDER]
    not_first = jnp.logical_or(me > 0, slab > 0)
    not_last = jnp.logical_or(me < N_INNER - 1, slab < N_SLAB - 1)

    barrier = pltpu.get_barrier_semaphore()
    for peer in peers:
        pl.semaphore_signal(barrier, inc=1, device_id=(slab, peer), device_id_type=MESH)
    for k in range(1, N_SLAB):

        @pl.when(slab >= k)
        def _():
            pl.semaphore_signal(barrier, inc=1, device_id=(slab - k, me), device_id_type=MESH)

    @pl.when(slab > 0)
    def _():
        pl.semaphore_signal(barrier, inc=1, device_id=(slab - 1, N_INNER - 1), device_id_type=MESH)

    small = [
        pltpu.make_async_copy(src, dst, psem.at[k])
        for k, (src, dst) in enumerate(
            [
                (dt_in, dt_ref),
                (wbc_in, wbc_ref),
                (bbc_in, bbc_ref),
                (bias_in, bias_ref),
                (alog_in, alog_ref),
                (skip_in, skip_ref),
                (wx_in, wx_ref),
                (bx_in, bx_ref),
            ]
        )
    ]
    own_bc = pltpu.make_async_copy(bc_ref, bcraw.at[pl.ds(EDGE, SPAN)], bsem)
    own_bc.start()
    for copy in small:
        copy.start()
    halo_out = jnp.logical_and(me == N_INNER - 1, slab < N_SLAB - 1)
    own_last = pltpu.make_async_copy(x_ref.at[pl.ds(SPAN - EDGE, EDGE)], xlast, lsem)

    @pl.when(halo_out)
    def _():
        own_last.start()

    pl.semaphore_wait(
        barrier, N_PEER + (N_SLAB - 1 - slab) + jnp.where(halo_out, N_INNER, 0)
    )

    def block(j):
        return pl.ds(pl.multiple_of(j * SPAN, SPAN), SPAN)

    def lanes_of(p):
        return slice(CUTS[p], CUTS[p + 1])

    def lane_ds(p):
        return pl.ds(CUTS[p], CUTS[p + 1] - CUTS[p])

    def x_cols(d, p):
        return pl.ds(pl.multiple_of(d * CH + CUTS[p], 128), CUTS[p + 1] - CUTS[p])

    def bc_cols(d, which):
        return pl.ds(pl.multiple_of((d // 2 + which * GROUPS) * STATE, STATE), STATE)

    def head_rows(d):
        return pl.ds(pl.multiple_of(d * NH, NH), NH)

    def remote(src, dst, send_sem, recv_sem, to):
        return pltpu.make_async_remote_copy(
            src, dst, send_sem, recv_sem, device_id=to, device_id_type=MESH
        )

    def landed(ref, sem):
        pltpu.make_async_copy(ref, ref, sem).wait()

    def bc_copy(n, which):
        return remote(
            bcconv.at[:, bc_cols(peers[n], which)], (bbuf, cbuf)[which].at[block(me)],
            ssend.at[which, n], srecv.at[which, me], (slab, peers[n]),
        )

    def dt_copy(n):
        return remote(
            dt_t.at[head_rows(peers[n])], dtbuf.at[me], ssend.at[2, n], srecv.at[2, me], (slab, peers[n])
        )

    def x_copy(n, p):
        return remote(
            x_ref.at[:, x_cols(peers[n], p)], xbuf.at[block(me), lane_ds(p)],
            xsend.at[p, n], xrecv.at[p, me], (slab, peers[n]),
        )

    def x_halo_copy(d):
        return remote(xpack.at[d], xhalo, hsend.at[d], hrecv, (slab + 1, d))

    def bc_halo_copy():
        wrap = me // (N_INNER - 1)
        return remote(bctail, bchalo, bhsend, bhrecv, (slab + wrap, (me + 1) * (1 - wrap)))

    def pack(rows, width):
        last = rows.astype(F32)[EDGE - 3 :]
        groups = rows.shape[1] // width
        return jnp.concatenate(
            [last[:, q * width : (q + 1) * width] for q in range(groups)]
            + [jnp.zeros((EDGE - 3 * groups, width), F32)],
            axis=0,
        ).astype(BF16)

    def unpack(packed, q):
        return jnp.concatenate(
            [jnp.zeros((EDGE - 3, packed.shape[1]), F32), packed.astype(F32)[3 * q : 3 * q + 3]], axis=0
        ).astype(BF16)

    own_bc.wait()
    bctail[...] = pack(bcraw[pl.ds(SPAN, EDGE), :], CH)

    @pl.when(not_last)
    def _():
        bc_halo_copy().start()

    for n in range(N_PEER):
        x_copy(n, 0).start()

    @pl.when(halo_out)
    def _():
        own_last.wait()

        @pl.loop(0, N_INNER)
        def _(d):
            xpack[d] = pack(xlast[:, pl.ds(pl.multiple_of(d * CH, CH), CH)], 256)
            x_halo_copy(d).start()

    for copy in small:
        copy.wait()
    dt_t[...] = dt_ref[...].astype(F32).T.astype(BF16)
    for n in range(N_PEER):
        dt_copy(n).start()

    own_dt = pltpu.make_async_copy(dt_t.at[head_rows(me)], dtbuf.at[me], srecv.at[2, me])
    own_dt.start()
    for p in range(PIECES):
        pltpu.make_async_copy(
            x_ref.at[:, x_cols(me, p)], xbuf.at[block(me), lane_ds(p)], xrecv.at[p, me]
        ).start()

    @pl.when(not_first)
    def _():
        landed(bchalo, bhrecv)
        for q in range(BC // CH):
            bcraw[pl.ds(0, EDGE), q * CH : (q + 1) * CH] = unpack(bchalo[...], q)

    @pl.when(jnp.logical_not(not_first))
    def _():
        bcraw[pl.ds(0, EDGE), :] = jnp.zeros((EDGE, BC), BF16)

    @pl.loop(0, BC // STATE)
    def _(g):
        cols = pl.ds(pl.multiple_of(g * STATE, STATE), STATE)
        weight, bias = wbc_ref[:, cols], bbc_ref[:, cols]
        for r in range(0, SPAN, SUB):
            bcconv[pl.ds(r, SUB), cols] = conv_silu(bcraw[pl.ds(r, SUB + EDGE), cols], weight, bias)

    for which in range(2):
        pltpu.make_async_copy(
            bcconv.at[:, bc_cols(me, which)], (bbuf, cbuf)[which].at[block(me)], srecv.at[which, me]
        ).start()
    for n in range(N_PEER):
        bc_copy(n, 0).start()
    for p in (1, 2):
        for n in range(N_PEER):
            x_copy(n, p).start()

    chan = lax.broadcasted_iota(jnp.int32, (128, CH), 1) // HEADDIM
    row = lax.broadcasted_iota(jnp.int32, (128, CH), 0)
    ew[...] = jnp.where((row < 2 * NH) & (lax.rem(row, NH) == chan), 1.0, 0.0).astype(BF16)
    ee[...] = jnp.where(
        (row >= 2 * NH) & (row < 4 * NH) & (lax.rem(row, NH) == chan), 1.0, 0.0
    ).astype(BF16)
    heads[...] = jnp.concatenate(
        [bias_ref[...], -jnp.exp(alog_ref[...]), skip_ref[...], jnp.zeros((5, HEADS), F32)], axis=0
    ).T
    own_heads = heads[head_rows(me), :]
    bias_col, rate_col, skip_col = own_heads[:, 0:1], own_heads[:, 1:2], own_heads[:, 2:3]
    pick = lax.broadcasted_iota(jnp.int32, (NH, CH), 0) == (
        lax.broadcasted_iota(jnp.int32, (NH, CH), 1) // HEADDIM
    )
    skip[...] = jnp.sum(jnp.where(pick, skip_col, 0.0), axis=0, keepdims=True)
    ep[0] = jnp.ones((1, CH), F32)
    row_ids = lax.broadcasted_iota(jnp.int32, (SPAN, SPAN), 0)
    col_ids = lax.broadcasted_iota(jnp.int32, (SPAN, SPAN), 1)
    upto = jnp.where(row_ids <= col_ids, 1.0, 0.0).astype(F32)

    @pl.loop(0, N_INNER)
    def _(j):
        landed(dtbuf.at[j], srecv.at[2, j])
        raw = dtbuf[j].astype(F32) + bias_col
        dt = jnp.maximum(raw, 0.0) + jnp.log1p(jnp.exp(-jnp.abs(raw)))
        da = dt * rate_col
        cumul = jnp.dot(da, upto, preferred_element_type=F32, precision=lax.Precision.HIGHEST)
        grow = jnp.exp(-cumul) * dt
        decay = jnp.exp(cumul)
        grow_hi = grow.astype(BF16).astype(F32)
        decay_hi = decay.astype(BF16).astype(F32)
        parts = jnp.concatenate(
            [grow_hi, grow - grow_hi, decay_hi, decay - decay_hi, jnp.zeros((4 * NH, SPAN), F32)],
            axis=0,
        )
        coef_j = parts.T.astype(BF16)
        coef[block(j), :] = coef_j
        dec_j = dot(coef_j[SPAN - EDGE :], ee[...])[EDGE - 1 : EDGE]
        dec[j] = dec_j
        ep[j + 1] = ep[j] * dec_j

    def tot_copy(k):
        return remote(ep.at[N_INNER], tot.at[slab], tsend.at[k], trecv.at[slab], (slab + k, me))

    for k in range(1, N_SLAB):

        @pl.when(slab + k < N_SLAB)
        def _():
            tot_copy(k).start()

    @pl.loop(0, slab)
    def _(m):
        landed(tot.at[m], trecv.at[m])

    @pl.loop(0, N_INNER)
    def _(j):
        landed(bbuf.at[block(j)], srecv.at[0, j])
        bt[block(j), :] = bbuf[block(j), :].astype(F32).T.astype(BF16)

    def end_copy(p, k):
        return remote(
            ebuf.at[:, lane_ds(p)], arr.at[slab, :, lane_ds(p)], esend.at[p, k], erecv.at[p, slab],
            (slab + k, me),
        )

    def gather_pass(p):
        lanes = lanes_of(p)
        own_cols = x_cols(me, p)
        width = CUTS[p + 1] - CUTS[p]
        carry[:, :width] = jnp.zeros((STATE, width), F32)

        if p == 0:

            @pl.when(slab > 0)
            def _():
                landed(xhalo, hrecv)
                for q in range(CH // 256):
                    edge[:, q * 256 : (q + 1) * 256] = unpack(xhalo[...], q)

            @pl.when(slab == 0)
            def _():
                edge[...] = jnp.zeros((EDGE, CH), BF16)

        @pl.loop(0, N_INNER)
        def _(j):
            landed(xbuf.at[block(j), lane_ds(p)], xrecv.at[p, j])
            weight, bias = wx_ref[:, own_cols], bx_ref[:, own_cols]
            before = edge[:, lanes]
            edge[:, lanes] = xbuf[pl.ds(pl.multiple_of((j + 1) * SPAN - EDGE, EDGE), EDGE), lanes]
            parts = []
            for r in reversed(range(0, SPAN, SUB)):
                at = pl.ds(pl.multiple_of(j * SPAN + r, SUB), SUB)
                if r:
                    rows = xbuf[pl.ds(pl.multiple_of(j * SPAN + r - EDGE, EDGE), SUB + EDGE), lanes]
                else:
                    rows = jnp.concatenate([before, xbuf[at, lanes]], axis=0)
                x_r = conv_silu(rows, weight, bias)
                xbuf[at, lanes] = x_r
                scaled = (x_r.astype(F32) * dot(coef[at, :], ew[:, lanes])).astype(BF16)
                xs[at, lanes] = scaled
                parts.insert(0, scaled)
            added = dot(bt[block(j), :], jnp.concatenate(parts, axis=0))
            now = carry[:, :width]
            state[j, :, lanes] = now
            carry[:, :width] = dec[j, :, lanes] * (now + added)

        ebuf[:, lanes] = carry[:, :width].astype(BF16)
        for k in range(1, N_SLAB):

            @pl.when(slab + k < N_SLAB)
            def _():
                end_copy(p, k).start()

    def incoming_pass(p):
        lanes = lanes_of(p)
        inc[:, lanes] = jnp.zeros((STATE, CUTS[p + 1] - CUTS[p]), F32)

        @pl.loop(0, slab)
        def _(m):
            landed(arr.at[m, :, lane_ds(p)], erecv.at[p, m])
            inc[:, lanes] = tot[m, :, lanes] * inc[:, lanes] + arr[m, :, lanes].astype(F32)

    for p in range(PIECES):
        gather_pass(p)
        if p in (0, 1):
            for n in range(N_PEER):
                x_copy(n, p + 3).start()
        if p == PIECES - 3:
            for n in range(C_EARLY):
                bc_copy(n, 1).start()
        if p == PIECES - 1:
            for n in range(C_EARLY, N_PEER):
                bc_copy(n, 1).start()
        if p:
            incoming_pass(p - 1)
    incoming_pass(PIECES - 1)

    def out_copy(j):
        return pltpu.make_async_copy(xs.at[block(j)], out_ref.at[block(j)], osem.at[j])

    @pl.loop(0, N_INNER)
    def _(i):
        j = me
        for n in range(N_PEER):
            j = jnp.where(i == n + 1, sources[n], j)
        landed(cbuf.at[block(j)], srecv.at[1, j])
        c_j = cbuf[block(j), :]
        g_j = jnp.where(row_ids >= col_ids, dot(c_j, bt[block(j), :]), 0.0).astype(BF16)
        for q in range(0, CH, 256):
            lanes = slice(q, q + 256)
            before = (state[j, :, lanes] + ep[j, :, lanes] * inc[:, lanes]).astype(BF16)
            acc = dot(g_j, xs[block(j), lanes]) + dot(c_j, before)
            acc = acc * dot(coef[block(j), :], ee[:, lanes])
            y = acc + skip[:, lanes] * xbuf[block(j), lanes].astype(F32)
            xs[block(j), lanes] = y.astype(BF16)
        out_copy(j).start()

    @pl.loop(0, N_INNER)
    def _(j):
        out_copy(j).wait()

    for n in range(N_PEER):
        bc_copy(n, 0).wait_send()
        bc_copy(n, 1).wait_send()
        dt_copy(n).wait_send()
        for p in range(PIECES):
            x_copy(n, p).wait_send()

    @pl.when(halo_out)
    def _():
        @pl.loop(0, N_INNER)
        def _(d):
            x_halo_copy(d).wait_send()

    @pl.when(not_last)
    def _():
        bc_halo_copy().wait_send()

    for k in range(1, N_SLAB):

        @pl.when(slab + k < N_SLAB)
        def _():
            tot_copy(k).wait_send()
            for p in range(PIECES):
                end_copy(p, k).wait_send()


def hand_over(y_ref, out_ref, buf, isem, osem):
    def at(j):
        return pl.ds(pl.multiple_of(j * PART, PART), PART)

    def read(j):
        return pltpu.make_async_copy(y_ref.at[at(j)], buf.at[at(j)], isem.at[j])

    def write(j):
        return pltpu.make_async_copy(buf.at[at(j)], out_ref.at[at(j)], osem.at[j])

    @pl.loop(0, N_PART)
    def _(j):
        read(j).start()

    @pl.loop(0, N_PART)
    def _(j):
        read(j).wait()
        write(j).start()

    @pl.loop(0, N_PART)
    def _(j):
        write(j).wait()


def shards(
    x_in, bc_in, dt_raw, dt_bias, a_log, d_skip, conv_x_weight, conv_x_bias, conv_bc_weight, conv_bc_bias
):
    tok_slab = N_INNER * SPAN
    anywhere = pl.BlockSpec(memory_space=pl.ANY)
    dma = pltpu.SemaphoreType.DMA
    y = pl.pallas_call(
        body,
        out_shape=jax.ShapeDtypeStruct((tok_slab, CH), BF16),
        in_specs=[anywhere] * 10,
        out_specs=anywhere,
        scratch_shapes=[
            pltpu.VMEM((SPAN, HEADS), BF16),
            pltpu.VMEM((1, HEADS), F32),
            pltpu.VMEM((1, HEADS), F32),
            pltpu.VMEM((1, HEADS), F32),
            pltpu.VMEM((4, N_INNER * CH), F32),
            pltpu.VMEM((1, N_INNER * CH), F32),
            pltpu.VMEM((4, BC), F32),
            pltpu.VMEM((1, BC), F32),
            dma((8,)),
            pltpu.VMEM((tok_slab, CH), BF16),
            pltpu.VMEM((EDGE, N_INNER * CH), BF16),
            pltpu.VMEM((N_INNER, EDGE, 256), BF16),
            pltpu.VMEM((EDGE, 256), BF16),
            pltpu.VMEM((EDGE, CH), BF16),
            pltpu.VMEM((EDGE + SPAN, BC), BF16),
            pltpu.VMEM((EDGE, CH), BF16),
            pltpu.VMEM((EDGE, CH), BF16),
            pltpu.VMEM((SPAN, BC), BF16),
            pltpu.VMEM((tok_slab, STATE), BF16),
            pltpu.VMEM((tok_slab, STATE), BF16),
            pltpu.VMEM((N_INNER, NH, SPAN), BF16),
            pltpu.VMEM((HEADS, SPAN), BF16),
            pltpu.VMEM((HEADS, 8), F32),
            pltpu.VMEM((tok_slab, SPAN), BF16),
            pltpu.VMEM((tok_slab, 128), BF16),
            pltpu.VMEM((128, CH), BF16),
            pltpu.VMEM((128, CH), BF16),
            pltpu.VMEM((N_INNER, 1, CH), F32),
            pltpu.VMEM((N_INNER + 1, 1, CH), F32),
            pltpu.VMEM((N_SLAB, 1, CH), F32),
            pltpu.VMEM((1, CH), F32),
            pltpu.VMEM((N_INNER, STATE, CH), F32),
            pltpu.VMEM((STATE, 256), F32),
            pltpu.VMEM((tok_slab, CH), BF16),
            pltpu.VMEM((STATE, CH), BF16),
            pltpu.VMEM((N_SLAB, STATE, CH), BF16),
            pltpu.VMEM((STATE, CH), F32),
            dma((PIECES, N_PEER)),
            dma((PIECES, N_INNER)),
            dma((3, N_PEER)),
            dma((3, N_INNER)),
            dma((N_INNER,)),
            dma,
            dma,
            dma,
            dma,
            dma,
            dma((N_SLAB,)),
            dma((N_SLAB,)),
            dma((PIECES, N_SLAB)),
            dma((PIECES, N_SLAB)),
            dma((N_INNER,)),
        ],
        compiler_params=pltpu.CompilerParams(
            collective_id=0, has_side_effects=True, vmem_limit_bytes=58 * 2**20
        ),
        cost_estimate=pl.CostEstimate(
            flops=9 * 10**9, bytes_accessed=18 * 2**20, transcendentals=6 * 2**20
        ),
    )(
        x_in,
        bc_in,
        dt_raw,
        dt_bias[None, :],
        a_log[None, :],
        d_skip[None, :],
        conv_x_weight,
        conv_x_bias[None, :],
        conv_bc_weight,
        conv_bc_bias[None, :],
    )
    return pl.pallas_call(
        hand_over,
        out_shape=jax.ShapeDtypeStruct((tok_slab, CH), BF16),
        in_specs=[anywhere],
        out_specs=anywhere,
        scratch_shapes=[pltpu.VMEM((tok_slab, CH), BF16), dma((N_PART,)), dma((N_PART,))],
        compiler_params=pltpu.CompilerParams(vmem_limit_bytes=56 * 2**20),
        cost_estimate=pl.CostEstimate(flops=0, bytes_accessed=16 * 2**20, transcendentals=0),
    )(y)


def solution(mesh):
    rows = P(("slab", "inner"), None)
    return jax.shard_map(
        shards,
        mesh=mesh,
        in_specs=(rows, rows, rows) + (P(),) * 7,
        out_specs=P("slab", "inner"),
        check_vma=False,
    )
```

```python
import jax
import jax.numpy as jnp
from jax import lax
from jax.experimental import pallas as pl
from jax.experimental.pallas import tpu as pltpu
from jax.sharding import PartitionSpec as P

HEADS = 256
HEADDIM = 64
STATE = 256
GROUPS = 8
SPAN = 256
N_SLAB = 8
N_INNER = 16
CH = 1024
NH = 16
CUTS = (0, 256, 512, 768, 896, 1024)
PIECES = len(CUTS) - 1
BC = 2 * GROUPS * STATE
C_EARLY = 8
EDGE = 16
PART = 512
N_PART = 8
SUB = 64
MESH = pl.DeviceIdType.MESH
ORDER = (
    (2, 2), (1, 0), (0, 3), (3, 1), (2, 1), (0, 1), (3, 0), (1, 3),
    (1, 2), (2, 0), (3, 3), (0, 2), (1, 1), (2, 3), (3, 2),
)
N_PEER = len(ORDER)
F32 = jnp.float32
BF16 = jnp.bfloat16


def dot(a, b):
    return jnp.dot(a, b, preferred_element_type=F32)


def conv_silu(rows, weight, bias):
    full = rows.astype(F32)
    n = rows.shape[0] - EDGE
    acc = bias
    for k in range(4):
        start = EDGE - 3 + k
        acc = acc + weight[k : k + 1, :] * full[start : start + n]
    half = 0.5 * acc
    return (half + half * jnp.tanh(half)).astype(BF16)


def body(
    x_ref, bc_ref, dt_in, bias_in, alog_in, skip_in, wx_in, bx_in, wbc_in, bbc_in,
    out_ref,
    dt_ref, bias_ref, alog_ref, skip_ref, wx_ref, bx_ref, wbc_ref, bbc_ref, psem,
    xbuf, xlast, xpack, xhalo, edge, bcraw, bctail, bchalo, bcconv, bbuf, cbuf, dtbuf, dt_t, heads, bt, coef, ew, ee, dec, ep, tot, skip,
    state, carry, xs, ebuf, arr, inc,
    xsend, xrecv, ssend, srecv, hsend, hrecv, bhsend, bhrecv, bsem, lsem, tsend, trecv, esend, erecv, osem,
):
    slab = lax.axis_index("slab")
    me = lax.axis_index("inner")
    my_z, my_x = me // 4, lax.rem(me, 4)
    sign = 1 - 2 * lax.rem(slab, 2)

    def at_offset(dx, dz, way):
        return lax.rem(my_z + way * dz + 4, 4) * 4 + lax.rem(my_x + way * dx + 4, 4)

    peers = [at_offset(dx, dz, sign) for dx, dz in ORDER]
    sources = [at_offset(dx, dz, -sign) for dx, dz in ORDER]
    not_first = jnp.logical_or(me > 0, slab > 0)
    not_last = jnp.logical_or(me < N_INNER - 1, slab < N_SLAB - 1)

    barrier = pltpu.get_barrier_semaphore()
    for peer in peers:
        pl.semaphore_signal(barrier, inc=1, device_id=(slab, peer), device_id_type=MESH)
    for k in range(1, N_SLAB):

        @pl.when(slab >= k)
        def _():
            pl.semaphore_signal(barrier, inc=1, device_id=(slab - k, me), device_id_type=MESH)

    @pl.when(slab > 0)
    def _():
        pl.semaphore_signal(barrier, inc=1, device_id=(slab - 1, N_INNER - 1), device_id_type=MESH)

    small = [
        pltpu.make_async_copy(src, dst, psem.at[k])
        for k, (src, dst) in enumerate(
            [
                (dt_in, dt_ref),
                (wbc_in, wbc_ref),
                (bbc_in, bbc_ref),
                (bias_in, bias_ref),
                (alog_in, alog_ref),
                (skip_in, skip_ref),
                (wx_in, wx_ref),
                (bx_in, bx_ref),
            ]
        )
    ]
    own_bc = pltpu.make_async_copy(bc_ref, bcraw.at[pl.ds(EDGE, SPAN)], bsem)
    own_bc.start()
    for copy in small:
        copy.start()
    halo_out = jnp.logical_and(me == N_INNER - 1, slab < N_SLAB - 1)
    own_last = pltpu.make_async_copy(x_ref.at[pl.ds(SPAN - EDGE, EDGE)], xlast, lsem)

    @pl.when(halo_out)
    def _():
        own_last.start()

    pl.semaphore_wait(
        barrier, N_PEER + (N_SLAB - 1 - slab) + jnp.where(halo_out, N_INNER, 0)
    )

    def block(j):
        return pl.ds(pl.multiple_of(j * SPAN, SPAN), SPAN)

    def lanes_of(p):
        return slice(CUTS[p], CUTS[p + 1])

    def lane_ds(p):
        return pl.ds(CUTS[p], CUTS[p + 1] - CUTS[p])

    def x_cols(d, p):
        return pl.ds(pl.multiple_of(d * CH + CUTS[p], 128), CUTS[p + 1] - CUTS[p])

    def bc_cols(d, which):
        return pl.ds(pl.multiple_of((d // 2 + which * GROUPS) * STATE, STATE), STATE)

    def head_rows(d):
        return pl.ds(pl.multiple_of(d * NH, NH), NH)

    def remote(src, dst, send_sem, recv_sem, to):
        return pltpu.make_async_remote_copy(
            src, dst, send_sem, recv_sem, device_id=to, device_id_type=MESH
        )

    def landed(ref, sem):
        pltpu.make_async_copy(ref, ref, sem).wait()

    def bc_copy(n, which):
        return remote(
            bcconv.at[:, bc_cols(peers[n], which)], (bbuf, cbuf)[which].at[block(me)],
            ssend.at[which, n], srecv.at[which, me], (slab, peers[n]),
        )

    def dt_copy(n):
        return remote(
            dt_t.at[head_rows(peers[n])], dtbuf.at[me], ssend.at[2, n], srecv.at[2, me], (slab, peers[n])
        )

    def x_copy(n, p):
        return remote(
            x_ref.at[:, x_cols(peers[n], p)], xbuf.at[block(me), lane_ds(p)],
            xsend.at[p, n], xrecv.at[p, me], (slab, peers[n]),
        )

    def x_halo_copy(d):
        return remote(xpack.at[d], xhalo, hsend.at[d], hrecv, (slab + 1, d))

    def bc_halo_copy():
        wrap = me // (N_INNER - 1)
        return remote(bctail, bchalo, bhsend, bhrecv, (slab + wrap, (me + 1) * (1 - wrap)))

    def pack(rows, width):
        last = rows.astype(F32)[EDGE - 3 :]
        groups = rows.shape[1] // width
        return jnp.concatenate(
            [last[:, q * width : (q + 1) * width] for q in range(groups)]
            + [jnp.zeros((EDGE - 3 * groups, width), F32)],
            axis=0,
        ).astype(BF16)

    def unpack(packed, q):
        return jnp.concatenate(
            [jnp.zeros((EDGE - 3, packed.shape[1]), F32), packed.astype(F32)[3 * q : 3 * q + 3]], axis=0
        ).astype(BF16)

    for n in range(4):
        x_copy(n, 0).start()

    own_bc.wait()
    bctail[...] = pack(bcraw[pl.ds(SPAN, EDGE), :], CH)

    @pl.when(not_last)
    def _():
        bc_halo_copy().start()

    for n in range(4, N_PEER):
        x_copy(n, 0).start()

    @pl.when(halo_out)
    def _():
        own_last.wait()

        @pl.loop(0, N_INNER)
        def _(d):
            xpack[d] = pack(xlast[:, pl.ds(pl.multiple_of(d * CH, CH), CH)], 256)
            x_halo_copy(d).start()

    for copy in small:
        copy.wait()
    dt_t[...] = dt_ref[...].astype(F32).T.astype(BF16)
    for n in range(N_PEER):
        dt_copy(n).start()

    own_dt = pltpu.make_async_copy(dt_t.at[head_rows(me)], dtbuf.at[me], srecv.at[2, me])
    own_dt.start()
    for p in range(PIECES):
        pltpu.make_async_copy(
            x_ref.at[:, x_cols(me, p)], xbuf.at[block(me), lane_ds(p)], xrecv.at[p, me]
        ).start()

    @pl.when(not_first)
    def _():
        landed(bchalo, bhrecv)
        for q in range(BC // CH):
            bcraw[pl.ds(0, EDGE), q * CH : (q + 1) * CH] = unpack(bchalo[...], q)

    @pl.when(jnp.logical_not(not_first))
    def _():
        bcraw[pl.ds(0, EDGE), :] = jnp.zeros((EDGE, BC), BF16)

    @pl.loop(0, BC // STATE)
    def _(g):
        cols = pl.ds(pl.multiple_of(g * STATE, STATE), STATE)
        weight, bias = wbc_ref[:, cols], bbc_ref[:, cols]
        for r in range(0, SPAN, SUB):
            bcconv[pl.ds(r, SUB), cols] = conv_silu(bcraw[pl.ds(r, SUB + EDGE), cols], weight, bias)

    for which in range(2):
        pltpu.make_async_copy(
            bcconv.at[:, bc_cols(me, which)], (bbuf, cbuf)[which].at[block(me)], srecv.at[which, me]
        ).start()
    for n in range(N_PEER):
        bc_copy(n, 0).start()
    for p in (1, 2):
        for n in range(N_PEER):
            x_copy(n, p).start()

    chan = lax.broadcasted_iota(jnp.int32, (128, CH), 1) // HEADDIM
    row = lax.broadcasted_iota(jnp.int32, (128, CH), 0)
    ew[...] = jnp.where((row < 2 * NH) & (lax.rem(row, NH) == chan), 1.0, 0.0).astype(BF16)
    ee[...] = jnp.where(
        (row >= 2 * NH) & (row < 4 * NH) & (lax.rem(row, NH) == chan), 1.0, 0.0
    ).astype(BF16)
    heads[...] = jnp.concatenate(
        [bias_ref[...], -jnp.exp(alog_ref[...]), skip_ref[...], jnp.zeros((5, HEADS), F32)], axis=0
    ).T
    own_heads = heads[head_rows(me), :]
    bias_col, rate_col, skip_col = own_heads[:, 0:1], own_heads[:, 1:2], own_heads[:, 2:3]
    pick = lax.broadcasted_iota(jnp.int32, (NH, CH), 0) == (
        lax.broadcasted_iota(jnp.int32, (NH, CH), 1) // HEADDIM
    )
    skip[...] = jnp.sum(jnp.where(pick, skip_col, 0.0), axis=0, keepdims=True)
    ep[0] = jnp.ones((1, CH), F32)
    row_ids = lax.broadcasted_iota(jnp.int32, (SPAN, SPAN), 0)
    col_ids = lax.broadcasted_iota(jnp.int32, (SPAN, SPAN), 1)
    upto = jnp.where(row_ids <= col_ids, 1.0, 0.0).astype(F32)

    @pl.loop(0, N_INNER)
    def _(j):
        landed(dtbuf.at[j], srecv.at[2, j])
        raw = dtbuf[j].astype(F32) + bias_col
        dt = jnp.maximum(raw, 0.0) + jnp.log1p(jnp.exp(-jnp.abs(raw)))
        da = dt * rate_col
        cumul = jnp.dot(da, upto, preferred_element_type=F32, precision=lax.Precision.HIGHEST)
        grow = jnp.exp(-cumul) * dt
        decay = jnp.exp(cumul)
        grow_hi = grow.astype(BF16).astype(F32)
        decay_hi = decay.astype(BF16).astype(F32)
        parts = jnp.concatenate(
            [grow_hi, grow - grow_hi, decay_hi, decay - decay_hi, jnp.zeros((4 * NH, SPAN), F32)],
            axis=0,
        )
        coef_j = parts.T.astype(BF16)
        coef[block(j), :] = coef_j
        dec_j = dot(coef_j[SPAN - EDGE :], ee[...])[EDGE - 1 : EDGE]
        dec[j] = dec_j
        ep[j + 1] = ep[j] * dec_j

    def tot_copy(k):
        return remote(ep.at[N_INNER], tot.at[slab], tsend.at[k], trecv.at[slab], (slab + k, me))

    for k in range(1, N_SLAB):

        @pl.when(slab + k < N_SLAB)
        def _():
            tot_copy(k).start()

    @pl.loop(0, slab)
    def _(m):
        landed(tot.at[m], trecv.at[m])

    @pl.loop(0, N_INNER)
    def _(j):
        landed(bbuf.at[block(j)], srecv.at[0, j])
        bt[block(j), :] = bbuf[block(j), :].astype(F32).T.astype(BF16)

    def end_copy(p, k):
        return remote(
            ebuf.at[:, lane_ds(p)], arr.at[slab, :, lane_ds(p)], esend.at[p, k], erecv.at[p, slab],
            (slab + k, me),
        )

    def gather_pass(p):
        lanes = lanes_of(p)
        own_cols = x_cols(me, p)
        width = CUTS[p + 1] - CUTS[p]
        carry[:, :width] = jnp.zeros((STATE, width), F32)

        if p == 0:

            @pl.when(slab > 0)
            def _():
                landed(xhalo, hrecv)
                for q in range(CH // 256):
                    edge[:, q * 256 : (q + 1) * 256] = unpack(xhalo[...], q)

            @pl.when(slab == 0)
            def _():
                edge[...] = jnp.zeros((EDGE, CH), BF16)

        @pl.loop(0, N_INNER)
        def _(j):
            landed(xbuf.at[block(j), lane_ds(p)], xrecv.at[p, j])
            weight, bias = wx_ref[:, own_cols], bx_ref[:, own_cols]
            before = edge[:, lanes]
            edge[:, lanes] = xbuf[pl.ds(pl.multiple_of((j + 1) * SPAN - EDGE, EDGE), EDGE), lanes]
            parts = []
            for r in reversed(range(0, SPAN, SUB)):
                at = pl.ds(pl.multiple_of(j * SPAN + r, SUB), SUB)
                if r:
                    rows = xbuf[pl.ds(pl.multiple_of(j * SPAN + r - EDGE, EDGE), SUB + EDGE), lanes]
                else:
                    rows = jnp.concatenate([before, xbuf[at, lanes]], axis=0)
                x_r = conv_silu(rows, weight, bias)
                xbuf[at, lanes] = x_r
                scaled = (x_r.astype(F32) * dot(coef[at, :], ew[:, lanes])).astype(BF16)
                xs[at, lanes] = scaled
                parts.insert(0, scaled)
            added = dot(bt[block(j), :], jnp.concatenate(parts, axis=0))
            now = carry[:, :width]
            state[j, :, lanes] = now
            carry[:, :width] = dec[j, :, lanes] * (now + added)

        ebuf[:, lanes] = carry[:, :width].astype(BF16)
        for k in range(1, N_SLAB):

            @pl.when(slab + k < N_SLAB)
            def _():
                end_copy(p, k).start()

    def incoming_pass(p):
        lanes = lanes_of(p)
        inc[:, lanes] = jnp.zeros((STATE, CUTS[p + 1] - CUTS[p]), F32)

        @pl.loop(0, slab)
        def _(m):
            landed(arr.at[m, :, lane_ds(p)], erecv.at[p, m])
            inc[:, lanes] = tot[m, :, lanes] * inc[:, lanes] + arr[m, :, lanes].astype(F32)

    for p in range(PIECES):
        gather_pass(p)
        if p in (0, 1):
            for n in range(N_PEER):
                x_copy(n, p + 3).start()
        if p == PIECES - 3:
            for n in range(C_EARLY):
                bc_copy(n, 1).start()
        if p == PIECES - 1:
            for n in range(C_EARLY, N_PEER):
                bc_copy(n, 1).start()
        if p:
            incoming_pass(p - 1)
    incoming_pass(PIECES - 1)

    def out_copy(j):
        return pltpu.make_async_copy(xs.at[block(j)], out_ref.at[block(j)], osem.at[j])

    @pl.loop(0, N_INNER)
    def _(i):
        j = me
        for n in range(N_PEER):
            j = jnp.where(i == n + 1, sources[n], j)
        landed(cbuf.at[block(j)], srecv.at[1, j])
        c_j = cbuf[block(j), :]
        g_j = jnp.where(row_ids >= col_ids, dot(c_j, bt[block(j), :]), 0.0).astype(BF16)
        for q in range(0, CH, 256):
            lanes = slice(q, q + 256)
            before = (state[j, :, lanes] + ep[j, :, lanes] * inc[:, lanes]).astype(BF16)
            acc = dot(g_j, xs[block(j), lanes]) + dot(c_j, before)
            acc = acc * dot(coef[block(j), :], ee[:, lanes])
            y = acc + skip[:, lanes] * xbuf[block(j), lanes].astype(F32)
            xs[block(j), lanes] = y.astype(BF16)
        out_copy(j).start()

    @pl.loop(0, N_INNER)
    def _(j):
        out_copy(j).wait()

    for n in range(N_PEER):
        bc_copy(n, 0).wait_send()
        bc_copy(n, 1).wait_send()
        dt_copy(n).wait_send()
        for p in range(PIECES):
            x_copy(n, p).wait_send()

    @pl.when(halo_out)
    def _():
        @pl.loop(0, N_INNER)
        def _(d):
            x_halo_copy(d).wait_send()

    @pl.when(not_last)
    def _():
        bc_halo_copy().wait_send()

    for k in range(1, N_SLAB):

        @pl.when(slab + k < N_SLAB)
        def _():
            tot_copy(k).wait_send()
            for p in range(PIECES):
                end_copy(p, k).wait_send()


def hand_over(y_ref, out_ref, buf, isem, osem):
    def at(j):
        return pl.ds(pl.multiple_of(j * PART, PART), PART)

    def read(j):
        return pltpu.make_async_copy(y_ref.at[at(j)], buf.at[at(j)], isem.at[j])

    def write(j):
        return pltpu.make_async_copy(buf.at[at(j)], out_ref.at[at(j)], osem.at[j])

    @pl.loop(0, N_PART)
    def _(j):
        read(j).start()

    @pl.loop(0, N_PART)
    def _(j):
        read(j).wait()
        write(j).start()

    @pl.loop(0, N_PART)
    def _(j):
        write(j).wait()


def shards(
    x_in, bc_in, dt_raw, dt_bias, a_log, d_skip, conv_x_weight, conv_x_bias, conv_bc_weight, conv_bc_bias
):
    tok_slab = N_INNER * SPAN
    anywhere = pl.BlockSpec(memory_space=pl.ANY)
    dma = pltpu.SemaphoreType.DMA
    y = pl.pallas_call(
        body,
        out_shape=jax.ShapeDtypeStruct((tok_slab, CH), BF16),
        in_specs=[anywhere] * 10,
        out_specs=anywhere,
        scratch_shapes=[
            pltpu.VMEM((SPAN, HEADS), BF16),
            pltpu.VMEM((1, HEADS), F32),
            pltpu.VMEM((1, HEADS), F32),
            pltpu.VMEM((1, HEADS), F32),
            pltpu.VMEM((4, N_INNER * CH), F32),
            pltpu.VMEM((1, N_INNER * CH), F32),
            pltpu.VMEM((4, BC), F32),
            pltpu.VMEM((1, BC), F32),
            dma((8,)),
            pltpu.VMEM((tok_slab, CH), BF16),
            pltpu.VMEM((EDGE, N_INNER * CH), BF16),
            pltpu.VMEM((N_INNER, EDGE, 256), BF16),
            pltpu.VMEM((EDGE, 256), BF16),
            pltpu.VMEM((EDGE, CH), BF16),
            pltpu.VMEM((EDGE + SPAN, BC), BF16),
            pltpu.VMEM((EDGE, CH), BF16),
            pltpu.VMEM((EDGE, CH), BF16),
            pltpu.VMEM((SPAN, BC), BF16),
            pltpu.VMEM((tok_slab, STATE), BF16),
            pltpu.VMEM((tok_slab, STATE), BF16),
            pltpu.VMEM((N_INNER, NH, SPAN), BF16),
            pltpu.VMEM((HEADS, SPAN), BF16),
            pltpu.VMEM((HEADS, 8), F32),
            pltpu.VMEM((tok_slab, SPAN), BF16),
            pltpu.VMEM((tok_slab, 128), BF16),
            pltpu.VMEM((128, CH), BF16),
            pltpu.VMEM((128, CH), BF16),
            pltpu.VMEM((N_INNER, 1, CH), F32),
            pltpu.VMEM((N_INNER + 1, 1, CH), F32),
            pltpu.VMEM((N_SLAB, 1, CH), F32),
            pltpu.VMEM((1, CH), F32),
            pltpu.VMEM((N_INNER, STATE, CH), F32),
            pltpu.VMEM((STATE, 256), F32),
            pltpu.VMEM((tok_slab, CH), BF16),
            pltpu.VMEM((STATE, CH), BF16),
            pltpu.VMEM((N_SLAB, STATE, CH), BF16),
            pltpu.VMEM((STATE, CH), F32),
            dma((PIECES, N_PEER)),
            dma((PIECES, N_INNER)),
            dma((3, N_PEER)),
            dma((3, N_INNER)),
            dma((N_INNER,)),
            dma,
            dma,
            dma,
            dma,
            dma,
            dma((N_SLAB,)),
            dma((N_SLAB,)),
            dma((PIECES, N_SLAB)),
            dma((PIECES, N_SLAB)),
            dma((N_INNER,)),
        ],
        compiler_params=pltpu.CompilerParams(
            collective_id=0, has_side_effects=True, vmem_limit_bytes=58 * 2**20
        ),
        cost_estimate=pl.CostEstimate(
            flops=9 * 10**9, bytes_accessed=18 * 2**20, transcendentals=6 * 2**20
        ),
    )(
        x_in,
        bc_in,
        dt_raw,
        dt_bias[None, :],
        a_log[None, :],
        d_skip[None, :],
        conv_x_weight,
        conv_x_bias[None, :],
        conv_bc_weight,
        conv_bc_bias[None, :],
    )
    return pl.pallas_call(
        hand_over,
        out_shape=jax.ShapeDtypeStruct((tok_slab, CH), BF16),
        in_specs=[anywhere],
        out_specs=anywhere,
        scratch_shapes=[pltpu.VMEM((tok_slab, CH), BF16), dma((N_PART,)), dma((N_PART,))],
        compiler_params=pltpu.CompilerParams(vmem_limit_bytes=56 * 2**20),
        cost_estimate=pl.CostEstimate(flops=0, bytes_accessed=16 * 2**20, transcendentals=0),
    )(y)


def solution(mesh):
    rows = P(("slab", "inner"), None)
    return jax.shard_map(
        shards,
        mesh=mesh,
        in_specs=(rows, rows, rows) + (P(),) * 7,
        out_specs=P("slab", "inner"),
        check_vma=False,
    )
```

```python
import jax
import jax.numpy as jnp
from jax import lax
from jax.experimental import pallas as pl
from jax.experimental.pallas import tpu as pltpu
from jax.sharding import PartitionSpec as P

HEADS = 256
HEADDIM = 64
STATE = 256
GROUPS = 8
SPAN = 256
N_SLAB = 8
N_INNER = 16
CH = 1024
NH = 16
CUTS = (0, 256, 512, 768, 896, 1024)
PIECES = len(CUTS) - 1
BC = 2 * GROUPS * STATE
C_EARLY = 8
EDGE = 16
PART = 512
N_PART = 8
SUB = 64
MESH = pl.DeviceIdType.MESH
ORDER = (
    (2, 2), (1, 0), (0, 3), (3, 1), (2, 1), (0, 1), (3, 0), (1, 3),
    (1, 2), (2, 0), (3, 3), (0, 2), (1, 1), (2, 3), (3, 2),
)
N_PEER = len(ORDER)
F32 = jnp.float32
BF16 = jnp.bfloat16


def dot(a, b):
    return jnp.dot(a, b, preferred_element_type=F32)


def conv_silu(rows, weight, bias):
    full = rows.astype(F32)
    n = rows.shape[0] - EDGE
    acc = bias
    for k in range(4):
        start = EDGE - 3 + k
        acc = acc + weight[k : k + 1, :] * full[start : start + n]
    half = 0.5 * acc
    return (half + half * jnp.tanh(half)).astype(BF16)


def body(
    x_ref, bc_ref, dt_in, bias_in, alog_in, skip_in, wx_in, bx_in, wbc_in, bbc_in,
    out_ref,
    dt_ref, bias_ref, alog_ref, skip_ref, wx_ref, bx_ref, wbc_ref, bbc_ref, psem,
    xbuf, xlast, xpack, xhalo, edge, bcraw, bctail, bchalo, bcconv, bbuf, cbuf, dtbuf, dt_t, heads, bt, coef, ew, ee, dec, ep, tot, skip,
    state, carry, xs, ebuf, arr, inc,
    xsend, xrecv, ssend, srecv, hsend, hrecv, bhsend, bhrecv, bsem, lsem, tsend, trecv, esend, erecv, osem,
):
    slab = lax.axis_index("slab")
    me = lax.axis_index("inner")
    my_z, my_x = me // 4, lax.rem(me, 4)
    sign = 1 - 2 * lax.rem(slab, 2)

    def at_offset(dx, dz, way):
        return lax.rem(my_z + way * dz + 4, 4) * 4 + lax.rem(my_x + way * dx + 4, 4)

    peers = [at_offset(dx, dz, sign) for dx, dz in ORDER]
    sources = [at_offset(dx, dz, -sign) for dx, dz in ORDER]
    not_first = jnp.logical_or(me > 0, slab > 0)
    not_last = jnp.logical_or(me < N_INNER - 1, slab < N_SLAB - 1)

    barrier = pltpu.get_barrier_semaphore()
    for peer in peers:
        pl.semaphore_signal(barrier, inc=1, device_id=(slab, peer), device_id_type=MESH)
    for k in range(1, N_SLAB):

        @pl.when(slab >= k)
        def _():
            pl.semaphore_signal(barrier, inc=1, device_id=(slab - k, me), device_id_type=MESH)

    @pl.when(slab > 0)
    def _():
        pl.semaphore_signal(barrier, inc=1, device_id=(slab - 1, N_INNER - 1), device_id_type=MESH)

    small = [
        pltpu.make_async_copy(src, dst, psem.at[k])
        for k, (src, dst) in enumerate(
            [
                (dt_in, dt_ref),
                (wbc_in, wbc_ref),
                (bbc_in, bbc_ref),
                (bias_in, bias_ref),
                (alog_in, alog_ref),
                (skip_in, skip_ref),
                (wx_in, wx_ref),
                (bx_in, bx_ref),
            ]
        )
    ]
    own_bc = pltpu.make_async_copy(bc_ref, bcraw.at[pl.ds(EDGE, SPAN)], bsem)
    own_bc.start()
    for copy in small:
        copy.start()
    halo_out = jnp.logical_and(me == N_INNER - 1, slab < N_SLAB - 1)
    own_last = pltpu.make_async_copy(x_ref.at[pl.ds(SPAN - EDGE, EDGE)], xlast, lsem)

    @pl.when(halo_out)
    def _():
        own_last.start()

    pl.semaphore_wait(
        barrier, N_PEER + (N_SLAB - 1 - slab) + jnp.where(halo_out, N_INNER, 0)
    )

    def block(j):
        return pl.ds(pl.multiple_of(j * SPAN, SPAN), SPAN)

    def lanes_of(p):
        return slice(CUTS[p], CUTS[p + 1])

    def lane_ds(p):
        return pl.ds(CUTS[p], CUTS[p + 1] - CUTS[p])

    def x_cols(d, p):
        return pl.ds(pl.multiple_of(d * CH + CUTS[p], 128), CUTS[p + 1] - CUTS[p])

    def bc_cols(d, which):
        return pl.ds(pl.multiple_of((d // 2 + which * GROUPS) * STATE, STATE), STATE)

    def head_rows(d):
        return pl.ds(pl.multiple_of(d * NH, NH), NH)

    def remote(src, dst, send_sem, recv_sem, to):
        return pltpu.make_async_remote_copy(
            src, dst, send_sem, recv_sem, device_id=to, device_id_type=MESH
        )

    def landed(ref, sem):
        pltpu.make_async_copy(ref, ref, sem).wait()

    def bc_copy(n, which):
        return remote(
            bcconv.at[:, bc_cols(peers[n], which)], (bbuf, cbuf)[which].at[block(me)],
            ssend.at[which, n], srecv.at[which, me], (slab, peers[n]),
        )

    def dt_copy(n):
        return remote(
            dt_t.at[head_rows(peers[n])], dtbuf.at[me], ssend.at[2, n], srecv.at[2, me], (slab, peers[n])
        )

    def x_copy(n, p):
        return remote(
            x_ref.at[:, x_cols(peers[n], p)], xbuf.at[block(me), lane_ds(p)],
            xsend.at[p, n], xrecv.at[p, me], (slab, peers[n]),
        )

    def x_halo_copy(d):
        return remote(xpack.at[d], xhalo, hsend.at[d], hrecv, (slab + 1, d))

    def bc_halo_copy():
        wrap = me // (N_INNER - 1)
        return remote(bctail, bchalo, bhsend, bhrecv, (slab + wrap, (me + 1) * (1 - wrap)))

    def pack(rows, width):
        last = rows.astype(F32)[EDGE - 3 :]
        groups = rows.shape[1] // width
        return jnp.concatenate(
            [last[:, q * width : (q + 1) * width] for q in range(groups)]
            + [jnp.zeros((EDGE - 3 * groups, width), F32)],
            axis=0,
        ).astype(BF16)

    def unpack(packed, q):
        return jnp.concatenate(
            [jnp.zeros((EDGE - 3, packed.shape[1]), F32), packed.astype(F32)[3 * q : 3 * q + 3]], axis=0
        ).astype(BF16)

    for n in range(4):
        x_copy(n, 0).start()

    own_bc.wait()
    bctail[...] = pack(bcraw[pl.ds(SPAN, EDGE), :], CH)

    @pl.when(not_last)
    def _():
        bc_halo_copy().start()

    for n in range(4, N_PEER):
        x_copy(n, 0).start()

    @pl.when(halo_out)
    def _():
        own_last.wait()

        @pl.loop(0, N_INNER)
        def _(d):
            xpack[d] = pack(xlast[:, pl.ds(pl.multiple_of(d * CH, CH), CH)], 256)
            x_halo_copy(d).start()

    for copy in small:
        copy.wait()
    dt_t[...] = dt_ref[...].astype(F32).T.astype(BF16)
    for n in range(N_PEER):
        dt_copy(n).start()

    own_dt = pltpu.make_async_copy(dt_t.at[head_rows(me)], dtbuf.at[me], srecv.at[2, me])
    own_dt.start()
    for p in range(PIECES):
        pltpu.make_async_copy(
            x_ref.at[:, x_cols(me, p)], xbuf.at[block(me), lane_ds(p)], xrecv.at[p, me]
        ).start()

    @pl.when(not_first)
    def _():
        landed(bchalo, bhrecv)
        for q in range(BC // CH):
            bcraw[pl.ds(0, EDGE), q * CH : (q + 1) * CH] = unpack(bchalo[...], q)

    @pl.when(jnp.logical_not(not_first))
    def _():
        bcraw[pl.ds(0, EDGE), :] = jnp.zeros((EDGE, BC), BF16)

    @pl.loop(0, BC // STATE)
    def _(g):
        cols = pl.ds(pl.multiple_of(g * STATE, STATE), STATE)
        weight, bias = wbc_ref[:, cols], bbc_ref[:, cols]
        for r in range(0, SPAN, SUB):
            bcconv[pl.ds(r, SUB), cols] = conv_silu(bcraw[pl.ds(r, SUB + EDGE), cols], weight, bias)

    for which in range(2):
        pltpu.make_async_copy(
            bcconv.at[:, bc_cols(me, which)], (bbuf, cbuf)[which].at[block(me)], srecv.at[which, me]
        ).start()
    for n in range(N_PEER):
        bc_copy(n, 0).start()
    for p in (1, 2):
        for n in range(N_PEER):
            x_copy(n, p).start()

    chan = lax.broadcasted_iota(jnp.int32, (128, CH), 1) // HEADDIM
    row = lax.broadcasted_iota(jnp.int32, (128, CH), 0)
    ew[...] = jnp.where((row < 2 * NH) & (lax.rem(row, NH) == chan), 1.0, 0.0).astype(BF16)
    ee[...] = jnp.where(
        (row >= 2 * NH) & (row < 4 * NH) & (lax.rem(row, NH) == chan), 1.0, 0.0
    ).astype(BF16)
    heads[...] = jnp.concatenate(
        [bias_ref[...], -jnp.exp(alog_ref[...]), skip_ref[...], jnp.zeros((5, HEADS), F32)], axis=0
    ).T
    own_heads = heads[head_rows(me), :]
    bias_col, rate_col, skip_col = own_heads[:, 0:1], own_heads[:, 1:2], own_heads[:, 2:3]
    pick = lax.broadcasted_iota(jnp.int32, (NH, CH), 0) == (
        lax.broadcasted_iota(jnp.int32, (NH, CH), 1) // HEADDIM
    )
    skip[...] = jnp.sum(jnp.where(pick, skip_col, 0.0), axis=0, keepdims=True)
    ep[0] = jnp.ones((1, CH), F32)
    row_ids = lax.broadcasted_iota(jnp.int32, (SPAN, SPAN), 0)
    col_ids = lax.broadcasted_iota(jnp.int32, (SPAN, SPAN), 1)
    upto = jnp.where(row_ids <= col_ids, 1.0, 0.0).astype(F32)

    @pl.loop(0, N_INNER)
    def _(j):
        landed(dtbuf.at[j], srecv.at[2, j])
        raw = dtbuf[j].astype(F32) + bias_col
        dt = jnp.maximum(raw, 0.0) + jnp.log1p(jnp.exp(-jnp.abs(raw)))
        da = dt * rate_col
        cumul = jnp.dot(da, upto, preferred_element_type=F32, precision=lax.Precision.HIGHEST)
        grow = jnp.exp(-cumul) * dt
        decay = jnp.exp(cumul)
        grow_hi = grow.astype(BF16).astype(F32)
        decay_hi = decay.astype(BF16).astype(F32)
        parts = jnp.concatenate(
            [grow_hi, grow - grow_hi, decay_hi, decay - decay_hi, jnp.zeros((4 * NH, SPAN), F32)],
            axis=0,
        )
        coef_j = parts.T.astype(BF16)
        coef[block(j), :] = coef_j
        dec_j = dot(coef_j[SPAN - EDGE :], ee[...])[EDGE - 1 : EDGE]
        dec[j] = dec_j
        ep[j + 1] = ep[j] * dec_j

    def tot_copy(k):
        return remote(ep.at[N_INNER], tot.at[slab], tsend.at[k], trecv.at[slab], (slab + k, me))

    for k in range(1, N_SLAB):

        @pl.when(slab + k < N_SLAB)
        def _():
            tot_copy(k).start()

    @pl.loop(0, slab)
    def _(m):
        landed(tot.at[m], trecv.at[m])

    @pl.loop(0, N_INNER)
    def _(j):
        landed(bbuf.at[block(j)], srecv.at[0, j])
        bt[block(j), :] = bbuf[block(j), :].astype(F32).T.astype(BF16)

    def end_copy(p, k):
        return remote(
            ebuf.at[:, lane_ds(p)], arr.at[slab, :, lane_ds(p)], esend.at[p, k], erecv.at[p, slab],
            (slab + k, me),
        )

    def gather_pass(p):
        lanes = lanes_of(p)
        own_cols = x_cols(me, p)
        width = CUTS[p + 1] - CUTS[p]
        carry[:, :width] = jnp.zeros((STATE, width), F32)

        if p == 0:

            @pl.when(slab > 0)
            def _():
                landed(xhalo, hrecv)
                for q in range(CH // 256):
                    edge[:, q * 256 : (q + 1) * 256] = unpack(xhalo[...], q)

            @pl.when(slab == 0)
            def _():
                edge[...] = jnp.zeros((EDGE, CH), BF16)

        @pl.loop(0, N_INNER)
        def _(j):
            landed(xbuf.at[block(j), lane_ds(p)], xrecv.at[p, j])
            weight, bias = wx_ref[:, own_cols], bx_ref[:, own_cols]
            before = edge[:, lanes]
            edge[:, lanes] = xbuf[pl.ds(pl.multiple_of((j + 1) * SPAN - EDGE, EDGE), EDGE), lanes]
            parts = []
            for r in reversed(range(0, SPAN, SUB)):
                at = pl.ds(pl.multiple_of(j * SPAN + r, SUB), SUB)
                if r:
                    rows = xbuf[pl.ds(pl.multiple_of(j * SPAN + r - EDGE, EDGE), SUB + EDGE), lanes]
                else:
                    rows = jnp.concatenate([before, xbuf[at, lanes]], axis=0)
                x_r = conv_silu(rows, weight, bias)
                xbuf[at, lanes] = x_r
                scaled = (x_r.astype(F32) * dot(coef[at, :], ew[:, lanes])).astype(BF16)
                xs[at, lanes] = scaled
                parts.insert(0, scaled)
            added = dot(bt[block(j), :], jnp.concatenate(parts, axis=0))
            now = carry[:, :width]
            state[j, :, lanes] = now
            carry[:, :width] = dec[j, :, lanes] * (now + added)

        ebuf[:, lanes] = carry[:, :width].astype(BF16)
        for k in range(1, N_SLAB):

            @pl.when(slab + k < N_SLAB)
            def _():
                end_copy(p, k).start()

    def incoming_pass(p):
        lanes = lanes_of(p)
        inc[:, lanes] = jnp.zeros((STATE, CUTS[p + 1] - CUTS[p]), F32)

        @pl.loop(0, slab)
        def _(m):
            landed(arr.at[m, :, lane_ds(p)], erecv.at[p, m])
            inc[:, lanes] = tot[m, :, lanes] * inc[:, lanes] + arr[m, :, lanes].astype(F32)

    for p in range(PIECES):
        gather_pass(p)
        if p in (0, 1):
            for n in range(N_PEER):
                x_copy(n, p + 3).start()
        if p == PIECES - 3:
            for n in range(C_EARLY):
                bc_copy(n, 1).start()
        if p == PIECES - 1:
            for n in range(C_EARLY, N_PEER):
                bc_copy(n, 1).start()
        if p:
            incoming_pass(p - 1)
    incoming_pass(PIECES - 1)

    def out_copy(j, half):
        at = pl.ds(half * (CH // 2), CH // 2)
        return pltpu.make_async_copy(
            xs.at[block(j), at], out_ref.at[block(j), at], osem.at[half, j]
        )

    @pl.loop(0, N_INNER)
    def _(i):
        j = me
        for n in range(N_PEER):
            j = jnp.where(i == n + 1, sources[n], j)
        landed(cbuf.at[block(j)], srecv.at[1, j])
        c_j = cbuf[block(j), :]
        g_j = jnp.where(row_ids >= col_ids, dot(c_j, bt[block(j), :]), 0.0).astype(BF16)
        for q in range(0, CH, 256):
            lanes = slice(q, q + 256)
            before = (state[j, :, lanes] + ep[j, :, lanes] * inc[:, lanes]).astype(BF16)
            acc = dot(g_j, xs[block(j), lanes]) + dot(c_j, before)
            acc = acc * dot(coef[block(j), :], ee[:, lanes])
            y = acc + skip[:, lanes] * xbuf[block(j), lanes].astype(F32)
            xs[block(j), lanes] = y.astype(BF16)
            if (q + 256) % (CH // 2) == 0:
                out_copy(j, q // (CH // 2)).start()

    @pl.loop(0, N_INNER)
    def _(j):
        out_copy(j, 0).wait()
        out_copy(j, 1).wait()

    for n in range(N_PEER):
        bc_copy(n, 0).wait_send()
        bc_copy(n, 1).wait_send()
        dt_copy(n).wait_send()
        for p in range(PIECES):
            x_copy(n, p).wait_send()

    @pl.when(halo_out)
    def _():
        @pl.loop(0, N_INNER)
        def _(d):
            x_halo_copy(d).wait_send()

    @pl.when(not_last)
    def _():
        bc_halo_copy().wait_send()

    for k in range(1, N_SLAB):

        @pl.when(slab + k < N_SLAB)
        def _():
            tot_copy(k).wait_send()
            for p in range(PIECES):
                end_copy(p, k).wait_send()


def hand_over(y_ref, out_ref, buf, isem, osem):
    def at(j):
        return pl.ds(pl.multiple_of(j * PART, PART), PART)

    def read(j):
        return pltpu.make_async_copy(y_ref.at[at(j)], buf.at[at(j)], isem.at[j])

    def write(j):
        return pltpu.make_async_copy(buf.at[at(j)], out_ref.at[at(j)], osem.at[j])

    @pl.loop(0, N_PART)
    def _(j):
        read(j).start()

    @pl.loop(0, N_PART)
    def _(j):
        read(j).wait()
        write(j).start()

    @pl.loop(0, N_PART)
    def _(j):
        write(j).wait()


def shards(
    x_in, bc_in, dt_raw, dt_bias, a_log, d_skip, conv_x_weight, conv_x_bias, conv_bc_weight, conv_bc_bias
):
    tok_slab = N_INNER * SPAN
    anywhere = pl.BlockSpec(memory_space=pl.ANY)
    dma = pltpu.SemaphoreType.DMA
    y = pl.pallas_call(
        body,
        out_shape=jax.ShapeDtypeStruct((tok_slab, CH), BF16),
        in_specs=[anywhere] * 10,
        out_specs=anywhere,
        scratch_shapes=[
            pltpu.VMEM((SPAN, HEADS), BF16),
            pltpu.VMEM((1, HEADS), F32),
            pltpu.VMEM((1, HEADS), F32),
            pltpu.VMEM((1, HEADS), F32),
            pltpu.VMEM((4, N_INNER * CH), F32),
            pltpu.VMEM((1, N_INNER * CH), F32),
            pltpu.VMEM((4, BC), F32),
            pltpu.VMEM((1, BC), F32),
            dma((8,)),
            pltpu.VMEM((tok_slab, CH), BF16),
            pltpu.VMEM((EDGE, N_INNER * CH), BF16),
            pltpu.VMEM((N_INNER, EDGE, 256), BF16),
            pltpu.VMEM((EDGE, 256), BF16),
            pltpu.VMEM((EDGE, CH), BF16),
            pltpu.VMEM((EDGE + SPAN, BC), BF16),
            pltpu.VMEM((EDGE, CH), BF16),
            pltpu.VMEM((EDGE, CH), BF16),
            pltpu.VMEM((SPAN, BC), BF16),
            pltpu.VMEM((tok_slab, STATE), BF16),
            pltpu.VMEM((tok_slab, STATE), BF16),
            pltpu.VMEM((N_INNER, NH, SPAN), BF16),
            pltpu.VMEM((HEADS, SPAN), BF16),
            pltpu.VMEM((HEADS, 8), F32),
            pltpu.VMEM((tok_slab, SPAN), BF16),
            pltpu.VMEM((tok_slab, 128), BF16),
            pltpu.VMEM((128, CH), BF16),
            pltpu.VMEM((128, CH), BF16),
            pltpu.VMEM((N_INNER, 1, CH), F32),
            pltpu.VMEM((N_INNER + 1, 1, CH), F32),
            pltpu.VMEM((N_SLAB, 1, CH), F32),
            pltpu.VMEM((1, CH), F32),
            pltpu.VMEM((N_INNER, STATE, CH), F32),
            pltpu.VMEM((STATE, 256), F32),
            pltpu.VMEM((tok_slab, CH), BF16),
            pltpu.VMEM((STATE, CH), BF16),
            pltpu.VMEM((N_SLAB, STATE, CH), BF16),
            pltpu.VMEM((STATE, CH), F32),
            dma((PIECES, N_PEER)),
            dma((PIECES, N_INNER)),
            dma((3, N_PEER)),
            dma((3, N_INNER)),
            dma((N_INNER,)),
            dma,
            dma,
            dma,
            dma,
            dma,
            dma((N_SLAB,)),
            dma((N_SLAB,)),
            dma((PIECES, N_SLAB)),
            dma((PIECES, N_SLAB)),
            dma((2, N_INNER)),
        ],
        compiler_params=pltpu.CompilerParams(
            collective_id=0, has_side_effects=True, vmem_limit_bytes=58 * 2**20
        ),
        cost_estimate=pl.CostEstimate(
            flops=9 * 10**9, bytes_accessed=18 * 2**20, transcendentals=6 * 2**20
        ),
    )(
        x_in,
        bc_in,
        dt_raw,
        dt_bias[None, :],
        a_log[None, :],
        d_skip[None, :],
        conv_x_weight,
        conv_x_bias[None, :],
        conv_bc_weight,
        conv_bc_bias[None, :],
    )
    return pl.pallas_call(
        hand_over,
        out_shape=jax.ShapeDtypeStruct((tok_slab, CH), BF16),
        in_specs=[anywhere],
        out_specs=anywhere,
        scratch_shapes=[pltpu.VMEM((tok_slab, CH), BF16), dma((N_PART,)), dma((N_PART,))],
        compiler_params=pltpu.CompilerParams(vmem_limit_bytes=56 * 2**20),
        cost_estimate=pl.CostEstimate(flops=0, bytes_accessed=16 * 2**20, transcendentals=0),
    )(y)


def solution(mesh):
    rows = P(("slab", "inner"), None)
    return jax.shard_map(
        shards,
        mesh=mesh,
        in_specs=(rows, rows, rows) + (P(),) * 7,
        out_specs=P("slab", "inner"),
        check_vma=False,
    )
```
